32 devices in a mesh: tour: 8 (over y, x, core), width: 4 (over z).
Axes of the slice: x: 2, y: 2, z: 4, core: 2. Of those that a mesh axis runs over, the one named last changes fastest.
Arguments:
- images: bfloat16 [2048, 1152], P('tour', 'width'), may hold values from -1.1953125 to 1.1953125
- texts: bfloat16 [2048, 1152], P('tour', 'width'), may hold values from -1.1953125 to 1.1953125
- matches: int32 [8, 256], P('tour'), may hold values from 0 to 255, each once within a row
- scale: float32 [1], replicated, may hold values from 0.7 to 2.5
- shift_bias: float32 [1], replicated, may hold values from -3 to 0
Outputs:
- grad_images: float32 [2048, 1152], P('tour', 'width')
- grad_texts: float32 [2048, 1152], P('tour', 'width')
The draws below stay inside these ranges and needn't reach their ends.
All inputs are finite; a program needn't handle non-finite values.
Results may differ from the reference program's by a relative error of at most 0.0025.
Values may be sent and summed in bfloat16 or wider, within the bound.
A program may use at most 64 MiB of HBM per device.

```python
import math
import jax
import jax.numpy as jnp
from jax import lax

D = 1152
B = 256
REACH = 7
BLOCKS = 8
ROWS = 2048


def block_levels(stream_key, dims, shards, smallest, high):
    gain, own = 1.0, jax.random.fold_in(stream_key, 6)
    for axis_at, shards_of in shards:
        draws = jnp.exp(jax.random.uniform(jax.random.fold_in(own, axis_at), (shards_of,), jnp.float32, smallest / len(shards), high / len(shards)))
        gain = gain * jnp.repeat(draws, dims[axis_at] // shards_of).reshape([-1 if axis == axis_at else 1 for axis in range(len(dims))])
    return gain


def scatter_about(key, dims, width, most, split=(), kind=jnp.bfloat16):
    values = jax.random.normal(key, dims, jnp.float32) * width
    if len(split) > 0:
        values = block_levels(key, dims, split, -0.22, 0.18) * values
    return jnp.clip(values, min=-most, max=most).astype(kind)


def setup_inputs(seed: int = 0) -> dict:
    seeds = jax.random.split(jax.random.key(seed), 6)
    images = scatter_about(seeds[0], (ROWS, D), 0.17, 1.1953125, ((0, 8), (1, 4)))
    texts = scatter_about(seeds[1], (ROWS, D), 0.17, 1.1953125, ((0, 8), (1, 4)))
    matches = jax.vmap(lambda own: jax.random.permutation(own, B))(jax.random.split(seeds[2], BLOCKS)).reshape((BLOCKS, B)).astype(jnp.int32)
    scale = jnp.clip(jnp.exp(jax.random.uniform(seeds[3], (1,), jnp.float32, math.log(0.7), math.log(2.5))), 0.7, 2.5)
    shift_bias = jnp.clip(jax.random.uniform(seeds[4], (1,), jnp.float32, -3.0, 0.0), -3.0, 0.0)
    return dict(images=images, texts=texts, matches=matches, scale=scale, shift_bias=shift_bias)


def reference(images, texts, matches, scale, shift_bias):
    temper = scale[0]
    offset_bias = shift_bias[0]
    image_blocks = images.reshape(BLOCKS, B, D).astype(jnp.float32)
    text_blocks = texts.reshape(BLOCKS, B, D).astype(jnp.float32)
    columns = jnp.arange(B, dtype=jnp.int32)
    positive = (matches[:, :, None] == columns[None, None, :]).astype(jnp.float32)
    grad_image = jnp.zeros((BLOCKS, B, D), jnp.float32)
    grad_text = jnp.zeros((BLOCKS, B, D), jnp.float32)
    for offset in range(-REACH, REACH + 1):
        other = jnp.roll(text_blocks, offset, axis=0)
        logits = temper * jnp.einsum("nad,ncd->nac", image_blocks, other) + offset_bias
        probs = jax.nn.sigmoid(logits)
        if offset == 0:
            probs = probs - positive
        weights = lax.optimization_barrier(probs.astype(jnp.bfloat16)).astype(jnp.float32)
        grad_image = grad_image + jnp.einsum("nac,ncd->nad", weights, other)
        grad_text = grad_text + jnp.roll(jnp.einsum("nac,nad->ncd", weights, image_blocks), -offset, axis=0)
    return (temper * grad_image).reshape(ROWS, D), (temper * grad_text).reshape(ROWS, D)
```

```python
import jax
import jax.numpy as jnp
from jax import lax
from jax.sharding import PartitionSpec as P

REACH = 7


def shifted(block, axis, distance):
    devices = range(lax.axis_size(axis))
    route = [((i - distance) % len(devices), i) for i in devices]
    return lax.ppermute(block, axis, route)


def cross_rows(left, right):
    return lax.dot_general(
        left, right, (((1,), (1,)), ((), ())), preferred_element_type=jnp.float32
    )


def cross_cols(weights, right):
    return lax.dot_general(
        weights, right, (((0,), (0,)), ((), ())), preferred_element_type=jnp.float32
    )


def band(images, texts, matches, scale, shift_bias):
    temper = scale[0]
    offset_bias = shift_bias[0]
    rows = images.shape[0]
    columns = lax.broadcasted_iota(jnp.int32, (rows, rows), 1)
    positive = (columns == matches[0][:, None]).astype(jnp.float32)

    def to_weights(total, label):
        probs = jax.nn.sigmoid(temper * total + offset_bias)
        if label is not None:
            probs = probs - label
        return probs.astype(jnp.bfloat16)

    def finish(parts, labels):
        totals = lax.psum(parts, "width")
        return tuple((to_weights(total, label) for total, label in zip(totals, labels)))

    own = finish((cross_rows(images, texts),), (positive,))[0]
    grad_image = jnp.dot(own, texts, preferred_element_type=jnp.float32)
    grad_text = cross_cols(own, images)
    for step in range(1, REACH + 1):
        lower = shifted(texts, "tour", step)
        upper = shifted(texts, "tour", -step)
        weight_low, weight_up = finish(
            (cross_rows(images, lower), cross_rows(images, upper)), (None, None)
        )
        grad_image = grad_image + jnp.dot(weight_low, lower, preferred_element_type=jnp.float32)
        grad_image = grad_image + jnp.dot(weight_up, upper, preferred_element_type=jnp.float32)
        back_low = shifted(cross_cols(weight_low, images), "tour", -step)
        back_up = shifted(cross_cols(weight_up, images), "tour", step)
        grad_text = grad_text + back_low + back_up
    return (temper * grad_image, temper * grad_text)


def whole(images, texts, matches, scale, shift_bias):
    n = lax.axis_size("tour")
    rows = images.shape[0]
    temper = scale[0]
    me = lax.axis_index("tour")
    gathered = lax.all_gather(texts, "tour", axis=0, tiled=True)
    total = lax.psum(cross_rows(images, gathered), "width")
    column = lax.broadcasted_iota(jnp.int32, total.shape, 1)
    hit = column == matches[0][:, None] + me * rows
    probs = jax.nn.sigmoid(temper * total + shift_bias[0])
    weights = (probs - hit.astype(jnp.float32)).astype(jnp.bfloat16)
    away = (me - column // rows + n) % n
    times = jnp.ones(total.shape, jnp.bfloat16)
    for d in range(n):
        count = len([s for s in range(-REACH, REACH + 1) if s % n == d])
        times = jnp.where(away == d, jnp.bfloat16(count), times)
    weights = weights * times
    grad_image = jnp.dot(weights, gathered, preferred_element_type=jnp.float32)
    grad_text = lax.psum_scatter(
        cross_cols(weights, images), "tour", scatter_dimension=0, tiled=True
    )
    return (temper * grad_image, temper * grad_text)


def solution(mesh):
    placed = (P("tour", "width"), P("tour", "width"), P("tour", None), P(), P())
    body = whole if mesh.shape["tour"] <= 2 * REACH + 1 else band
    return jax.shard_map(
        body,
        mesh=mesh,
        in_specs=placed,
        out_specs=(P("tour", "width"), P("tour", "width")),
        check_vma=False,
    )
```

```python
import functools

import jax
import jax.numpy as jnp
from jax import lax
from jax.experimental import pallas as pl
from jax.experimental.pallas import tpu as pltpu
from jax.sharding import PartitionSpec as P

REACH = 7
MESH = pl.DeviceIdType.MESH


def shifted(block, axis, distance):
    devices = range(lax.axis_size(axis))
    route = [((i - distance) % len(devices), i) for i in devices]
    return lax.ppermute(block, axis, route)


def cross_rows(left, right):
    return lax.dot_general(
        left, right, (((1,), (1,)), ((), ())), preferred_element_type=jnp.float32
    )


def cross_cols(weights, right):
    return lax.dot_general(
        weights, right, (((0,), (0,)), ((), ())), preferred_element_type=jnp.float32
    )


def band(images, texts, matches, scale, shift_bias):
    temper = scale[0]
    offset_bias = shift_bias[0]
    rows = images.shape[0]
    columns = lax.broadcasted_iota(jnp.int32, (rows, rows), 1)
    positive = (columns == matches[0][:, None]).astype(jnp.float32)

    def to_weights(total, label):
        probs = jax.nn.sigmoid(temper * total + offset_bias)
        if label is not None:
            probs = probs - label
        return probs.astype(jnp.bfloat16)

    def finish(parts, labels):
        totals = lax.psum(parts, "width")
        return tuple((to_weights(total, label) for total, label in zip(totals, labels)))

    own = finish((cross_rows(images, texts),), (positive,))[0]
    grad_image = jnp.dot(own, texts, preferred_element_type=jnp.float32)
    grad_text = cross_cols(own, images)
    for step in range(1, REACH + 1):
        lower = shifted(texts, "tour", step)
        upper = shifted(texts, "tour", -step)
        weight_low, weight_up = finish(
            (cross_rows(images, lower), cross_rows(images, upper)), (None, None)
        )
        grad_image = grad_image + jnp.dot(weight_low, lower, preferred_element_type=jnp.float32)
        grad_image = grad_image + jnp.dot(weight_up, upper, preferred_element_type=jnp.float32)
        back_low = shifted(cross_cols(weight_low, images), "tour", -step)
        back_up = shifted(cross_cols(weight_up, images), "tour", step)
        grad_text = grad_text + back_low + back_up
    return (temper * grad_image, temper * grad_text)


def kernel(
    n, m, images, texts, matches, params, grad_image, grad_text,
    image_slabs, text_slabs, text_terms, text_got, image_terms, image_got, text_sums, text_final,
    quarter_send, quarter_recv, image_send, image_recv, plane_send, plane_recv,
    term_send, term_recv, back_send, back_recv, final_send, final_recv,
):
    t, z = lax.axis_index("tour"), lax.axis_index("width")
    rows, width = images.shape
    part = rows // m
    temper, offset_bias = params[0], params[1]

    def along(k):
        return lax.rem(t + k, n)

    def across(k):
        return lax.rem(z + k, m)

    def quarter(k):
        return pl.ds(pl.multiple_of(across(k) * part, part), part)

    def send(src, dst, send_sem, recv_sem, device):
        copy = pltpu.make_async_remote_copy(
            src_ref=src, dst_ref=dst, send_sem=send_sem, recv_sem=recv_sem,
            device_id=device, device_id_type=MESH,
        )
        copy.start()
        return copy

    barrier = pltpu.get_barrier_semaphore()
    for k in range(1, m):
        pl.semaphore_signal(barrier, inc=1, device_id={"width": across(k)}, device_id_type=MESH)
    for k in range(1, n):
        pl.semaphore_signal(barrier, inc=1, device_id={"tour": along(k)}, device_id_type=MESH)
    text_slabs[0, 0] = texts[quarter(0), :]
    pl.semaphore_wait(barrier, n + m - 2)

    sent = []
    quarters, slabs, plane = {}, {}, {}
    for k in range(1, m):
        e = m - k
        quarters[e] = send(
            texts.at[quarter(k)], text_slabs.at[0, e], quarter_send.at[e], quarter_recv.at[e],
            {"width": across(k)},
        )

    def spread(e):
        for k in range(1, n):
            d = n - k
            plane[d, e] = send(
                text_slabs.at[0, e], text_slabs.at[d, e], plane_send.at[d, e], plane_recv.at[d, e],
                {"tour": along(k)},
            )

    spread(0)
    for k in range(1, m):
        e = m - k
        slabs[e] = send(
            images, image_slabs.at[e - 1], image_send.at[e], image_recv.at[e], {"width": across(k)}
        )
    for e in range(1, m):
        quarters[e].wait_recv()
        spread(e)

    def image_slab(e):
        return images[...] if e == 0 else image_slabs[e - 1]

    def text_slab(e):
        return text_slabs[:, e].reshape(n * part, width)

    total = None
    for e in range(m):
        if e > 0:
            slabs[e].wait_recv()
        for d in range(1, n):
            plane[d, e].wait_recv()
        term = cross_rows(text_slab(e), image_slab(e))
        total = term if total is None else total + term
    probs = jax.nn.sigmoid(temper * total + offset_bias)
    place = lax.broadcasted_iota(jnp.int32, (part, rows), 0) + z * part
    label = (place == matches[...]).astype(jnp.float32)
    pieces = []
    for d in range(n):
        count = len([s for s in range(-REACH, REACH + 1) if (s + d) % n == 0])
        piece = probs[d * part : (d + 1) * part]
        if d == 0:
            piece = piece - label
        pieces.append(piece.astype(jnp.bfloat16).astype(jnp.float32) * count)
    weights = jnp.concatenate(pieces, axis=0)
    turned = weights.T.astype(jnp.bfloat16)
    weights = weights.astype(jnp.bfloat16)

    own = []
    for e in range(m):
        term = jnp.dot(weights, image_slab(e), preferred_element_type=jnp.float32)
        own.append(term[:part])
        for d in range(1, n):
            text_terms[d - 1, e] = term[d * part : (d + 1) * part].astype(jnp.bfloat16)
    terms, backs, finals = {}, {}, {}
    for d in range(1, n):
        terms[n - d] = send(
            text_terms.at[d - 1], text_got.at[n - d - 1], term_send.at[d], term_recv.at[n - d],
            {"tour": along(d)},
        )
    for e in range(1, m):
        term = jnp.dot(turned, text_slab(e), preferred_element_type=jnp.float32)
        image_terms[e - 1] = term.astype(jnp.bfloat16)
        backs[m - e] = send(
            image_terms.at[e - 1], image_got.at[m - e - 1], back_send.at[e], back_recv.at[m - e],
            {"width": across(e)},
        )
    kept = jnp.dot(turned, text_slab(0), preferred_element_type=jnp.float32)

    for d in range(1, n):
        terms[d].wait_recv()
    for e in list(range(1, m)) + [0]:
        value = own[e]
        for d in range(1, n):
            value = value + text_got[d - 1, e].astype(jnp.float32)
        value = temper * value
        if e == 0:
            grad_text[quarter(0), :] = value
        else:
            text_sums[e - 1] = value
            finals[m - e] = send(
                text_sums.at[e - 1], text_final.at[m - e - 1], final_send.at[e], final_recv.at[m - e],
                {"width": across(e)},
            )
    for e in range(1, m):
        backs[e].wait_recv()
        kept = kept + image_got[e - 1].astype(jnp.float32)
    grad_image[...] = temper * kept
    for e in range(1, m):
        finals[e].wait_recv()
        grad_text[quarter(e), :] = text_final[e - 1]
    for group in (quarters, slabs, plane, terms, backs, finals):
        for copy in group.values():
            copy.wait_send()


def whole(images, texts, matches, scale, shift_bias):
    n, m = lax.axis_size("tour"), lax.axis_size("width")
    rows, width = images.shape
    part = rows // m
    params = jnp.concatenate([scale, shift_bias])
    vmem = pl.BlockSpec(memory_space=pltpu.VMEM)
    dma = pltpu.SemaphoreType.DMA
    out = jax.ShapeDtypeStruct((rows, width), jnp.float32)
    return pl.pallas_call(
        functools.partial(kernel, n, m),
        out_shape=(out, out),
        in_specs=[vmem, vmem, vmem, pl.BlockSpec(memory_space=pltpu.SMEM)],
        out_specs=(vmem, vmem),
        scratch_shapes=[
            pltpu.VMEM((m - 1, rows, width), jnp.bfloat16),
            pltpu.VMEM((n, m, part, width), jnp.bfloat16),
            pltpu.VMEM((n - 1, m, part, width), jnp.bfloat16),
            pltpu.VMEM((n - 1, m, part, width), jnp.bfloat16),
            pltpu.VMEM((m - 1, rows, width), jnp.bfloat16),
            pltpu.VMEM((m - 1, rows, width), jnp.bfloat16),
            pltpu.VMEM((m - 1, part, width), jnp.float32),
            pltpu.VMEM((m - 1, part, width), jnp.float32),
            dma((m,)), dma((m,)), dma((m,)), dma((m,)), dma((n, m)), dma((n, m)),
            dma((n,)), dma((n,)), dma((m,)), dma((m,)), dma((m,)), dma((m,)),
        ],
        compiler_params=pltpu.CompilerParams(
            collective_id=0, has_side_effects=True, vmem_limit_bytes=48 * 1024 * 1024
        ),
    )(images, texts, matches, params)


def solution(mesh):
    placed = (P("tour", "width"), P("tour", "width"), P("tour", None), P(), P())
    body = whole if mesh.shape["tour"] <= 2 * REACH + 1 else band
    return jax.shard_map(
        body,
        mesh=mesh,
        in_specs=placed,
        out_specs=(P("tour", "width"), P("tour", "width")),
        check_vma=False,
    )
```

```python
import functools

import jax
import jax.numpy as jnp
from jax import lax
from jax.experimental import pallas as pl
from jax.experimental.pallas import tpu as pltpu
from jax.sharding import PartitionSpec as P

REACH = 7
MESH = pl.DeviceIdType.MESH


def shifted(block, axis, distance):
    devices = range(lax.axis_size(axis))
    route = [((i - distance) % len(devices), i) for i in devices]
    return lax.ppermute(block, axis, route)


def cross_rows(left, right):
    return lax.dot_general(
        left, right, (((1,), (1,)), ((), ())), preferred_element_type=jnp.float32
    )


def cross_cols(weights, right):
    return lax.dot_general(
        weights, right, (((0,), (0,)), ((), ())), preferred_element_type=jnp.float32
    )


def band(images, texts, matches, scale, shift_bias):
    temper = scale[0]
    offset_bias = shift_bias[0]
    rows = images.shape[0]
    columns = lax.broadcasted_iota(jnp.int32, (rows, rows), 1)
    positive = (columns == matches[0][:, None]).astype(jnp.float32)

    def to_weights(total, label):
        probs = jax.nn.sigmoid(temper * total + offset_bias)
        if label is not None:
            probs = probs - label
        return probs.astype(jnp.bfloat16)

    def finish(parts, labels):
        totals = lax.psum(parts, "width")
        return tuple((to_weights(total, label) for total, label in zip(totals, labels)))

    own = finish((cross_rows(images, texts),), (positive,))[0]
    grad_image = jnp.dot(own, texts, preferred_element_type=jnp.float32)
    grad_text = cross_cols(own, images)
    for step in range(1, REACH + 1):
        lower = shifted(texts, "tour", step)
        upper = shifted(texts, "tour", -step)
        weight_low, weight_up = finish(
            (cross_rows(images, lower), cross_rows(images, upper)), (None, None)
        )
        grad_image = grad_image + jnp.dot(weight_low, lower, preferred_element_type=jnp.float32)
        grad_image = grad_image + jnp.dot(weight_up, upper, preferred_element_type=jnp.float32)
        back_low = shifted(cross_cols(weight_low, images), "tour", -step)
        back_up = shifted(cross_cols(weight_up, images), "tour", step)
        grad_text = grad_text + back_low + back_up
    return (temper * grad_image, temper * grad_text)


def kernel(
    n, m, images, texts, matches, params, grad_image, grad_text,
    image_all, text_all, text_terms, term_got, text_got, text_own, text_sums, text_final,
    image_terms, image_got,
    quarter_send, quarter_recv, image_send, image_recv, plane_send, plane_recv, share_send,
    term_send, term_recv, hop_send, hop_recv, back_send, back_recv, final_send, final_recv,
):
    t, z = lax.axis_index("tour"), lax.axis_index("width")
    width, rows = images.shape
    cores = 2
    halves, chips = m // cores, n // cores
    half = rows // halves
    temper, offset_bias = params[0], params[1]
    core, chip = lax.rem(t, cores), lax.div(t, cores)
    plane_core, plane_half = lax.div(z, halves), lax.rem(z, halves)
    keeper = core == plane_core
    helper = core != plane_core
    sibling = chip * cores + (cores - 1 - core)
    slabs = [lax.rem(z + k, m) for k in range(m)]
    keepers = [lax.rem(chip + r, chips) * cores + plane_core for r in range(chips)]
    targets = [core * halves + h for h in range(halves)]
    elsewhere = [target != z for target in targets]
    everyone = z >= 0
    started = []

    def remote(src, dst, send_sem, recv_sem, device):
        return pltpu.make_async_remote_copy(
            src_ref=src, dst_ref=dst, send_sem=send_sem, recv_sem=recv_sem,
            device_id=device, device_id_type=MESH,
        )

    def arriving(dst, recv_sem):
        return remote(dst, dst, quarter_send.at[0], recv_sem, {"width": slabs[1]})

    quarter = [
        remote(
            texts.at[:, h * half : (h + 1) * half], text_all.at[0, z],
            quarter_send.at[h], quarter_recv.at[z], {"width": targets[h]},
        )
        for h in range(halves)
    ]
    image, image_in, quarter_in, back, back_in, final = {}, {}, {}, {}, {}, {}
    plane, plane_in, share, term_out, hop, hop_in = {}, {}, {}, {}, {}, {}
    for k in range(1, m):
        f = slabs[k]
        quarter_in[k] = arriving(text_all.at[0, f], quarter_recv.at[f])
        image[k] = remote(images, image_all.at[z], image_send.at[k], image_recv.at[z], {"width": f})
        image_in[k] = arriving(image_all.at[f], image_recv.at[f])
        back[k] = remote(
            image_terms.at[k - 1], image_got.at[z], back_send.at[k], back_recv.at[z], {"width": f}
        )
        back_in[k] = arriving(image_got.at[f], back_recv.at[f])
        final[k] = remote(
            text_sums.at[k - 1], text_final.at[plane_half],
            final_send.at[k], final_recv.at[plane_half], {"width": f},
        )
    final_in = [arriving(text_final.at[h], final_recv.at[h]) for h in range(halves)]
    for r in range(chips):
        for k in range(m):
            f = slabs[k]
            plane_in[r, k] = arriving(text_all.at[r, f], plane_recv.at[r, f])
            share[r, k] = remote(
                text_all.at[r, f], text_all.at[r, f], share_send.at[r, k], plane_recv.at[r, f],
                {"tour": sibling},
            )
            if r > 0:
                plane[r, k] = remote(
                    text_all.at[0, f], text_all.at[chips - r, f],
                    plane_send.at[r, k], plane_recv.at[chips - r, f], {"tour": keepers[r]},
                )
        term_out[r] = remote(
            text_terms.at[r], term_got.at[r], term_send.at[r], term_recv.at[r], {"tour": sibling}
        )
        if r > 0:
            hop[r] = remote(
                text_terms.at[r], text_got.at[chips - r - 1],
                hop_send.at[r], hop_recv.at[chips - r], {"tour": keepers[r]},
            )
            hop_in[r] = arriving(text_got.at[r - 1], hop_recv.at[r])

    barrier = pltpu.get_barrier_semaphore()
    for k in range(1, m):
        pl.semaphore_signal(barrier, inc=1, device_id={"width": slabs[k]}, device_id_type=MESH)
    for k in range(1, n):
        pl.semaphore_signal(
            barrier, inc=1, device_id={"tour": lax.rem(t + k, n)}, device_id_type=MESH
        )
    image_all[z] = images[...]
    for h in range(halves):
        @pl.when(targets[h] == z)
        def _():
            text_all[0, z] = texts[:, h * half : (h + 1) * half]
    spot = jnp.broadcast_to(matches[...].astype(jnp.float32), (half, rows)).T
    pl.semaphore_wait(barrier, n + m - 2)

    for h in range(halves):
        @pl.when(elsewhere[h])
        def _():
            quarter[h].start()
    for k in (2, 1, 3):
        image[k].start()

    @pl.when(keeper)
    def _():
        for k in range(m):
            if k > 0:
                quarter_in[k].wait_recv()
            for r in range(1, chips):
                plane[r, k].start()
            share[0, k].start()
        for k in range(m):
            for r in range(1, chips):
                plane_in[r, k].wait_recv()
                share[r, k].start()

    @pl.when(helper)
    def _():
        for k in range(m):
            for r in range(chips):
                plane_in[r, k].wait_recv()

    def text_slab(f):
        return jnp.concatenate([text_all[r, f] for r in range(chips)], axis=1)

    total = None
    for k in range(m):
        if k > 0:
            image_in[k].wait_recv()
        term = cross_cols(image_all[slabs[k]], text_slab(slabs[k]))
        total = term if total is None else total + term
    probs = jax.nn.sigmoid(temper * total + offset_bias)
    column = lax.broadcasted_iota(jnp.int32, (rows, half), 1) + plane_half * half
    hit = jnp.where(keeper, 1.0, 0.0) * (column.astype(jnp.float32) == spot).astype(jnp.float32)
    counts = [len([s for s in range(-REACH, REACH + 1) if s % n == d]) for d in range(n)]
    weights, turned = [], []
    for r in range(chips):
        piece = probs[:, r * half : (r + 1) * half]
        if r == 0:
            piece = piece - hit
        distance = lax.rem(t - keepers[r] + n, n)
        count = jnp.float32(0)
        for d in range(n):
            count = jnp.where(distance == d, jnp.float32(counts[d]), count)
        piece = piece.astype(jnp.bfloat16).astype(jnp.float32) * count
        weights.append(piece.astype(jnp.bfloat16))
        turned.append(piece.T.astype(jnp.bfloat16))
    turned = jnp.concatenate(turned, axis=0)

    image_rows = image_all[...].reshape(m * width, rows)
    for r in list(range(1, chips)) + [0]:
        term = jnp.dot(image_rows, weights[r], preferred_element_type=jnp.float32)

        @pl.when(helper)
        def _():
            text_terms[r] = term.astype(jnp.bfloat16)
            term_out[r].start()

        @pl.when(keeper)
        def _():
            term_out[r].wait_recv()
            both = term + term_got[r].astype(jnp.float32)
            if r == 0:
                text_own[...] = both
            else:
                text_terms[r] = both.astype(jnp.bfloat16)
                hop[r].start()

    for k in (2, 1, 3, 0):
        term = jnp.dot(text_slab(slabs[k]), turned, preferred_element_type=jnp.float32)
        if k == 0:
            kept = term
        else:
            image_terms[k - 1] = term.astype(jnp.bfloat16)
            back[k].start()

    @pl.when(keeper)
    def _():
        for r in range(1, chips):
            hop_in[r].wait_recv()
        for k in (2, 1, 3, 0):
            span = pl.ds(pl.multiple_of(slabs[k] * width, width), width)
            value = text_own[span, :]
            for r in range(1, chips):
                value = value + text_got[r - 1, span, :].astype(jnp.float32)
            value = temper * value
            if k == 0:
                text_final[plane_half] = value
            else:
                text_sums[k - 1] = value
                final[k].start()

    for k in range(1, m):
        back_in[k].wait_recv()
        kept = kept + image_got[slabs[k]].astype(jnp.float32)
    grad_image[...] = temper * kept
    for h in range(halves):
        @pl.when(elsewhere[h])
        def _():
            final_in[h].wait_recv()
            quarter[h].wait_send()
        grad_text[:, h * half : (h + 1) * half] = text_final[h]
    for group in (image, back):
        for copy in group.values():
            copy.wait_send()

    @pl.when(keeper)
    def _():
        for group in (plane, share, hop, final):
            for copy in group.values():
                copy.wait_send()

    @pl.when(helper)
    def _():
        for copy in term_out.values():
            copy.wait_send()


def whole(images, texts, matches, scale, shift_bias):
    n, m = lax.axis_size("tour"), lax.axis_size("width")
    rows, width = images.shape
    chips, half, full = n // 2, rows // (m // 2), m * width
    params = jnp.concatenate([scale, shift_bias])
    vmem = pl.BlockSpec(memory_space=pltpu.VMEM)
    out = jax.ShapeDtypeStruct((width, rows), jnp.float32)

    def dma(*shape):
        return pltpu.SemaphoreType.DMA(shape)

    grads = pl.pallas_call(
        functools.partial(kernel, n, m),
        out_shape=(out, out),
        in_specs=[vmem, vmem, vmem, pl.BlockSpec(memory_space=pltpu.SMEM)],
        out_specs=(vmem, vmem),
        scratch_shapes=[
            pltpu.VMEM((m, width, rows), jnp.bfloat16),
            pltpu.VMEM((chips, m, width, half), jnp.bfloat16),
            pltpu.VMEM((chips, full, half), jnp.bfloat16),
            pltpu.VMEM((chips, full, half), jnp.bfloat16),
            pltpu.VMEM((chips - 1, full, half), jnp.bfloat16),
            pltpu.VMEM((full, half), jnp.float32),
            pltpu.VMEM((m - 1, width, half), jnp.float32),
            pltpu.VMEM((m // 2, width, half), jnp.float32),
            pltpu.VMEM((m - 1, width, rows), jnp.bfloat16),
            pltpu.VMEM((m, width, rows), jnp.bfloat16),
            dma(m), dma(m), dma(m), dma(m), dma(chips, m), dma(chips, m), dma(chips, m),
            dma(chips), dma(chips), dma(chips), dma(chips), dma(m), dma(m), dma(m), dma(m),
        ],
        compiler_params=pltpu.CompilerParams(
            collective_id=0, has_side_effects=True, vmem_limit_bytes=48 * 1024 * 1024
        ),
    )(images.T, texts.T, matches, params)
    return tuple(grad.T for grad in grads)


def solution(mesh):
    placed = (P("tour", "width"), P("tour", "width"), P("tour", None), P(), P())
    n, m = mesh.shape["tour"], mesh.shape["width"]
    body = whole if n <= 2 * REACH + 1 and n % 2 == 0 and m == 4 else band
    return jax.shard_map(
        body,
        mesh=mesh,
        in_specs=placed,
        out_specs=(P("tour", "width"), P("tour", "width")),
        check_vma=False,
    )
```

```python
import functools

import jax
import jax.numpy as jnp
from jax import lax
from jax.experimental import pallas as pl
from jax.experimental.pallas import tpu as pltpu
from jax.sharding import PartitionSpec as P

REACH = 7
MESH = pl.DeviceIdType.MESH


def shifted(block, axis, distance):
    devices = range(lax.axis_size(axis))
    route = [((i - distance) % len(devices), i) for i in devices]
    return lax.ppermute(block, axis, route)


def cross_rows(left, right):
    return lax.dot_general(
        left, right, (((1,), (1,)), ((), ())), preferred_element_type=jnp.float32
    )


def cross_cols(weights, right):
    return lax.dot_general(
        weights, right, (((0,), (0,)), ((), ())), preferred_element_type=jnp.float32
    )


def band(images, texts, matches, scale, shift_bias):
    temper = scale[0]
    offset_bias = shift_bias[0]
    rows = images.shape[0]
    columns = lax.broadcasted_iota(jnp.int32, (rows, rows), 1)
    positive = (columns == matches[0][:, None]).astype(jnp.float32)

    def to_weights(total, label):
        probs = jax.nn.sigmoid(temper * total + offset_bias)
        if label is not None:
            probs = probs - label
        return probs.astype(jnp.bfloat16)

    def finish(parts, labels):
        totals = lax.psum(parts, "width")
        return tuple((to_weights(total, label) for total, label in zip(totals, labels)))

    own = finish((cross_rows(images, texts),), (positive,))[0]
    grad_image = jnp.dot(own, texts, preferred_element_type=jnp.float32)
    grad_text = cross_cols(own, images)
    for step in range(1, REACH + 1):
        lower = shifted(texts, "tour", step)
        upper = shifted(texts, "tour", -step)
        weight_low, weight_up = finish(
            (cross_rows(images, lower), cross_rows(images, upper)), (None, None)
        )
        grad_image = grad_image + jnp.dot(weight_low, lower, preferred_element_type=jnp.float32)
        grad_image = grad_image + jnp.dot(weight_up, upper, preferred_element_type=jnp.float32)
        back_low = shifted(cross_cols(weight_low, images), "tour", -step)
        back_up = shifted(cross_cols(weight_up, images), "tour", step)
        grad_text = grad_text + back_low + back_up
    return (temper * grad_image, temper * grad_text)


def kernel(
    n, m, images_in, texts_in, matches_in, params, grad_image, grad_text,
    texts, matches, image_all, text_all, text_terms, term_got, text_got, text_own, text_sums, text_final,
    image_terms, image_sums, image_got,
    load_sem, relay_send, quarter_send, quarter_recv, image_send, image_recv, plane_send, plane_recv, share_send,
    term_send, term_recv, hop_send, hop_recv, back_send, back_recv, final_send, final_recv,
):
    t, z = lax.axis_index("tour"), lax.axis_index("width")
    width, rows = texts.shape
    cores = 2
    halves, chips = m // cores, n // cores
    half = rows // halves
    temper, offset_bias = params[0], params[1]
    core, chip = lax.rem(t, cores), lax.div(t, cores)
    plane_core, plane_half = lax.div(z, halves), lax.rem(z, halves)
    keeper = core == plane_core
    helper = core != plane_core
    sibling = chip * cores + (cores - 1 - core)
    slabs = [lax.rem(z + k, m) for k in range(m)]
    keepers = [lax.rem(chip + r, chips) * cores + plane_core for r in range(chips)]
    targets = [core * halves + h for h in range(halves)]
    elsewhere = [target != z for target in targets]
    outer = jnp.logical_or(z == 0, z == m - 1)
    inner = jnp.logical_not(outer)
    low = z < halves
    partner = jnp.where(low, 1 - z, 2 * m - 3 - z)
    far_inner = jnp.where(low, halves, halves - 1)
    far_outer = jnp.where(low, m - 1, 0)
    direct = [jnp.logical_or(inner, f != far_outer) for f in slabs]

    loads = [
        pltpu.make_async_copy(images_in, image_all.at[z], load_sem.at[0]),
        pltpu.make_async_copy(texts_in, texts, load_sem.at[1]),
        pltpu.make_async_copy(matches_in, matches, load_sem.at[2]),
    ]
    for load in loads:
        load.start()

    def remote(src, dst, send_sem, recv_sem, device):
        return pltpu.make_async_remote_copy(
            src_ref=src, dst_ref=dst, send_sem=send_sem, recv_sem=recv_sem,
            device_id=device, device_id_type=MESH,
        )

    def arriving(dst, recv_sem):
        return remote(dst, dst, quarter_send.at[0], recv_sem, {"width": slabs[1]})

    quarter = [
        remote(
            texts.at[:, h * half : (h + 1) * half], text_all.at[0, z],
            quarter_send.at[h], quarter_recv.at[z], {"width": targets[h]},
        )
        for h in range(halves)
    ]
    image, image_in, quarter_in, final = {}, {}, {}, {}
    plane, plane_in, share, term_out, hop, hop_in = {}, {}, {}, {}, {}, {}
    for k in range(1, m):
        f = slabs[k]
        quarter_in[k] = arriving(text_all.at[0, f], quarter_recv.at[f])
        image[k] = remote(image_all.at[z], image_all.at[z], image_send.at[k], image_recv.at[z], {"width": f})
        image_in[k] = arriving(image_all.at[f], image_recv.at[f])
        final[k] = remote(
            text_sums.at[k - 1], text_final.at[plane_half],
            final_send.at[k], final_recv.at[plane_half], {"width": f},
        )
    relay = remote(
        image_all.at[far_outer], image_all.at[far_outer], relay_send.at[0], image_recv.at[far_outer],
        {"width": partner},
    )

    def back(i, slot, device):
        return remote(
            image_terms.at[i], image_got.at[slot], back_send.at[i], back_recv.at[slot],
            {"width": device},
        )

    near_out = back(2, 2, partner)
    outer_out = [back(0, 0, partner), back(1, 1, partner)]
    inner_out = [back(0, 3, far_outer), back(1, 3, far_inner)]
    back_in = [arriving(image_got.at[i], back_recv.at[i]) for i in range(4)]
    final_in = [arriving(text_final.at[h], final_recv.at[h]) for h in range(halves)]
    for r in range(chips):
        for k in range(m):
            f = slabs[k]
            plane_in[r, k] = arriving(text_all.at[r, f], plane_recv.at[r, f])
            share[r, k] = remote(
                text_all.at[r, f], text_all.at[r, f], share_send.at[r, k], plane_recv.at[r, f],
                {"tour": sibling},
            )
            if r > 0:
                plane[r, k] = remote(
                    text_all.at[0, f], text_all.at[chips - r, f],
                    plane_send.at[r, k], plane_recv.at[chips - r, f], {"tour": keepers[r]},
                )
        term_out[r] = remote(
            text_terms.at[r], term_got.at[r], term_send.at[r], term_recv.at[r], {"tour": sibling}
        )
        if r > 0:
            hop[r] = remote(
                text_terms.at[r], text_got.at[chips - r - 1],
                hop_send.at[r], hop_recv.at[chips - r], {"tour": keepers[r]},
            )
            hop_in[r] = arriving(text_got.at[r - 1], hop_recv.at[r])

    barrier = pltpu.get_barrier_semaphore()
    for k in range(1, m):
        pl.semaphore_signal(barrier, inc=1, device_id={"width": slabs[k]}, device_id_type=MESH)
    for k in range(1, n):
        pl.semaphore_signal(
            barrier, inc=1, device_id={"tour": lax.rem(t + k, n)}, device_id_type=MESH
        )
    for load in loads:
        load.wait()
    for h in range(halves):
        @pl.when(targets[h] == z)
        def _():
            text_all[0, z] = texts[:, h * half : (h + 1) * half]
    pl.semaphore_wait(barrier, n + m - 2)

    for h in range(halves):
        @pl.when(elsewhere[h])
        def _():
            quarter[h].start()
    for k in (2, 1, 3):
        @pl.when(direct[k])
        def _():
            image[k].start()
    spot = jnp.broadcast_to(matches[...].astype(jnp.float32), (half, rows)).T

    @pl.when(keeper)
    def _():
        for k in range(m):
            if k > 0:
                quarter_in[k].wait_recv()
            for r in range(1, chips):
                plane[r, k].start()
            share[0, k].start()

    @pl.when(inner)
    def _():
        image_in[2].wait_recv()
        relay.start()

    @pl.when(keeper)
    def _():
        for k in range(m):
            for r in range(1, chips):
                plane_in[r, k].wait_recv()
                share[r, k].start()

    @pl.when(helper)
    def _():
        for k in range(m):
            for r in range(chips):
                plane_in[r, k].wait_recv()

    def text_slab(f):
        return jnp.concatenate([text_all[r, f] for r in range(chips)], axis=1)

    total = None
    for k in range(m):
        if k == 2:
            @pl.when(outer)
            def _():
                image_in[2].wait_recv()
        elif k > 0:
            image_in[k].wait_recv()
        term = cross_cols(image_all[slabs[k]], text_slab(slabs[k]))
        total = term if total is None else total + term
    probs = jax.nn.sigmoid(temper * total + offset_bias)
    column = lax.broadcasted_iota(jnp.int32, (rows, half), 1) + plane_half * half
    hit = jnp.where(keeper, 1.0, 0.0) * (column.astype(jnp.float32) == spot).astype(jnp.float32)
    counts = [len([s for s in range(-REACH, REACH + 1) if s % n == d]) for d in range(n)]
    weights, turned = [], []
    for r in range(chips):
        piece = probs[:, r * half : (r + 1) * half]
        if r == 0:
            piece = piece - hit
        distance = lax.rem(t - keepers[r] + n, n)
        count = jnp.float32(0)
        for d in range(n):
            count = jnp.where(distance == d, jnp.float32(counts[d]), count)
        piece = piece.astype(jnp.bfloat16).astype(jnp.float32) * count
        weights.append(piece.astype(jnp.bfloat16))
        turned.append(piece.T.astype(jnp.bfloat16))
    turned = jnp.concatenate(turned, axis=0)

    def image_term(f):
        return jnp.dot(text_slab(f), turned, preferred_element_type=jnp.float32)

    for i, f in enumerate((far_outer, far_inner)):
        term = image_term(f)

        @pl.when(outer)
        def _():
            image_terms[i] = term.astype(jnp.bfloat16)
            outer_out[i].start()

        @pl.when(inner)
        def _():
            image_sums[i] = term

    image_terms[2] = image_term(partner).astype(jnp.bfloat16)
    near_out.start()
    kept = image_term(z)

    image_rows = image_all[...].reshape(m * width, rows)
    for r in list(range(1, chips)) + [0]:
        term = jnp.dot(image_rows, weights[r], preferred_element_type=jnp.float32)

        @pl.when(helper)
        def _():
            text_terms[r] = term.astype(jnp.bfloat16)
            term_out[r].start()

        @pl.when(keeper)
        def _():
            term_out[r].wait_recv()
            both = term + term_got[r].astype(jnp.float32)
            if r == 0:
                text_own[...] = both
            else:
                text_terms[r] = both.astype(jnp.bfloat16)
                hop[r].start()

    @pl.when(inner)
    def _():
        for i in range(2):
            back_in[i].wait_recv()
            value = image_sums[i] + image_got[i].astype(jnp.float32)
            image_terms[i] = value.astype(jnp.bfloat16)
            inner_out[i].start()

    @pl.when(keeper)
    def _():
        for r in range(1, chips):
            hop_in[r].wait_recv()
        for k in (2, 1, 3, 0):
            span = pl.ds(pl.multiple_of(slabs[k] * width, width), width)
            value = text_own[span, :]
            for r in range(1, chips):
                value = value + text_got[r - 1, span, :].astype(jnp.float32)
            value = temper * value
            if k == 0:
                text_final[plane_half] = value
            else:
                text_sums[k - 1] = value
                final[k].start()

    for i in (2, 3):
        back_in[i].wait_recv()
        kept = kept + image_got[i].astype(jnp.float32)
    grad_image[...] = temper * kept
    for h in range(halves):
        @pl.when(elsewhere[h])
        def _():
            final_in[h].wait_recv()
            quarter[h].wait_send()
        grad_text[:, h * half : (h + 1) * half] = text_final[h]
    for k in range(1, m):
        @pl.when(direct[k])
        def _():
            image[k].wait_send()
    near_out.wait_send()

    @pl.when(outer)
    def _():
        for copy in outer_out:
            copy.wait_send()

    @pl.when(inner)
    def _():
        for copy in [relay] + inner_out:
            copy.wait_send()

    @pl.when(keeper)
    def _():
        for group in (plane, share, hop, final):
            for copy in group.values():
                copy.wait_send()

    @pl.when(helper)
    def _():
        for copy in term_out.values():
            copy.wait_send()


def whole(images, texts, matches, scale, shift_bias):
    n, m = lax.axis_size("tour"), lax.axis_size("width")
    rows, width = images.shape
    chips, half, full = n // 2, rows // (m // 2), m * width
    params = jnp.concatenate([scale, shift_bias])
    hbm = pl.BlockSpec(memory_space=pltpu.HBM)
    vmem = pl.BlockSpec(memory_space=pltpu.VMEM)
    out = jax.ShapeDtypeStruct((width, rows), jnp.float32)

    def dma(*shape):
        return pltpu.SemaphoreType.DMA(shape)

    grads = pl.pallas_call(
        functools.partial(kernel, n, m),
        out_shape=(out, out),
        in_specs=[hbm, hbm, hbm, pl.BlockSpec(memory_space=pltpu.SMEM)],
        out_specs=(vmem, vmem),
        scratch_shapes=[
            pltpu.VMEM((width, rows), jnp.bfloat16),
            pltpu.VMEM((1, rows), jnp.int32),
            pltpu.VMEM((m, width, rows), jnp.bfloat16),
            pltpu.VMEM((chips, m, width, half), jnp.bfloat16),
            pltpu.VMEM((chips, full, half), jnp.bfloat16),
            pltpu.VMEM((chips, full, half), jnp.bfloat16),
            pltpu.VMEM((chips - 1, full, half), jnp.bfloat16),
            pltpu.VMEM((full, half), jnp.float32),
            pltpu.VMEM((m - 1, width, half), jnp.float32),
            pltpu.VMEM((m // 2, width, half), jnp.float32),
            pltpu.VMEM((3, width, rows), jnp.bfloat16),
            pltpu.VMEM((2, width, rows), jnp.float32),
            pltpu.VMEM((4, width, rows), jnp.bfloat16),
            dma(3), dma(1), dma(m), dma(m), dma(m), dma(m), dma(chips, m), dma(chips, m), dma(chips, m),
            dma(chips), dma(chips), dma(chips), dma(chips), dma(m), dma(m), dma(m), dma(m),
        ],
        compiler_params=pltpu.CompilerParams(
            collective_id=0, has_side_effects=True, vmem_limit_bytes=60 * 1024 * 1024
        ),
    )(images.T, texts.T, matches, params)
    return tuple(grad.T for grad in grads)


def solution(mesh):
    placed = (P("tour", "width"), P("tour", "width"), P("tour", None), P(), P())
    n, m = mesh.shape["tour"], mesh.shape["width"]
    body = whole if n <= 2 * REACH + 1 and n % 2 == 0 and m == 4 else band
    return jax.shard_map(
        body,
        mesh=mesh,
        in_specs=placed,
        out_specs=(P("tour", "width"), P("tour", "width")),
        check_vma=False,
    )
```

```python
import functools

import jax
import jax.numpy as jnp
from jax import lax
from jax.experimental import pallas as pl
from jax.experimental.pallas import tpu as pltpu
from jax.sharding import PartitionSpec as P

REACH = 7
MESH = pl.DeviceIdType.MESH


def shifted(block, axis, distance):
    devices = range(lax.axis_size(axis))
    route = [((i - distance) % len(devices), i) for i in devices]
    return lax.ppermute(block, axis, route)


def cross_rows(left, right):
    return lax.dot_general(
        left, right, (((1,), (1,)), ((), ())), preferred_element_type=jnp.float32
    )


def cross_cols(weights, right):
    return lax.dot_general(
        weights, right, (((0,), (0,)), ((), ())), preferred_element_type=jnp.float32
    )


def band(images, texts, matches, scale, shift_bias):
    temper = scale[0]
    offset_bias = shift_bias[0]
    rows = images.shape[0]
    columns = lax.broadcasted_iota(jnp.int32, (rows, rows), 1)
    positive = (columns == matches[0][:, None]).astype(jnp.float32)

    def to_weights(total, label):
        probs = jax.nn.sigmoid(temper * total + offset_bias)
        if label is not None:
            probs = probs - label
        return probs.astype(jnp.bfloat16)

    def finish(parts, labels):
        totals = lax.psum(parts, "width")
        return tuple((to_weights(total, label) for total, label in zip(totals, labels)))

    own = finish((cross_rows(images, texts),), (positive,))[0]
    grad_image = jnp.dot(own, texts, preferred_element_type=jnp.float32)
    grad_text = cross_cols(own, images)
    for step in range(1, REACH + 1):
        lower = shifted(texts, "tour", step)
        upper = shifted(texts, "tour", -step)
        weight_low, weight_up = finish(
            (cross_rows(images, lower), cross_rows(images, upper)), (None, None)
        )
        grad_image = grad_image + jnp.dot(weight_low, lower, preferred_element_type=jnp.float32)
        grad_image = grad_image + jnp.dot(weight_up, upper, preferred_element_type=jnp.float32)
        back_low = shifted(cross_cols(weight_low, images), "tour", -step)
        back_up = shifted(cross_cols(weight_up, images), "tour", step)
        grad_text = grad_text + back_low + back_up
    return (temper * grad_image, temper * grad_text)


def kernel(
    n, m, images_in, texts_in, matches_in, scale, shift_bias, grad_image, grad_text,
    texts, matches, image_all, text_all, text_terms, term_got, text_got, text_own, text_sums, text_final,
    image_terms, image_sums, image_got, image_final,
    load_sem, store_sem, relay_send, quarter_send, quarter_recv, image_send, image_recv,
    plane_send, plane_recv, share_send, term_send, term_recv, hop_send, hop_recv,
    back_send, back_recv, final_send, final_recv,
):
    t, z = lax.axis_index("tour"), lax.axis_index("width")
    width, rows = texts.shape
    cores = 2
    halves, chips = m // cores, n // cores
    half = rows // halves
    temper, offset_bias = scale[0], shift_bias[0]
    core, chip = lax.rem(t, cores), lax.div(t, cores)
    plane_core, plane_half = lax.div(z, halves), lax.rem(z, halves)
    keeper = core == plane_core
    helper = core != plane_core
    sibling = chip * cores + (cores - 1 - core)
    slabs = [lax.rem(z + k, m) for k in range(m)]
    keepers = [lax.rem(chip + r, chips) * cores + plane_core for r in range(chips)]
    targets = [core * halves + h for h in range(halves)]
    elsewhere = [target != z for target in targets]
    both_halves = range(halves)
    spans = [slice(p * half, (p + 1) * half) for p in both_halves]
    outer = jnp.logical_or(z == 0, z == m - 1)
    inner = jnp.logical_not(outer)
    low = z < halves
    partner = jnp.where(low, 1 - z, 2 * m - 3 - z)
    far_inner = jnp.where(low, halves, halves - 1)
    far_outer = jnp.where(low, m - 1, 0)
    direct = [jnp.logical_or(inner, f != far_outer) for f in slabs]
    order = (far_outer, far_inner, partner, z)

    loads = [
        pltpu.make_async_copy(images_in, image_all.at[z], load_sem.at[0]),
        pltpu.make_async_copy(texts_in, texts, load_sem.at[1]),
        pltpu.make_async_copy(matches_in, matches, load_sem.at[2]),
    ]
    for load in loads:
        load.start()

    def remote(src, dst, send_sem, recv_sem, device):
        return pltpu.make_async_remote_copy(
            src_ref=src, dst_ref=dst, send_sem=send_sem, recv_sem=recv_sem,
            device_id=device, device_id_type=MESH,
        )

    def arriving(dst, recv_sem):
        return remote(dst, dst, quarter_send.at[0], recv_sem, {"width": slabs[1]})

    quarter = [
        remote(
            texts.at[:, spans[h]], text_all.at[0, z],
            quarter_send.at[h], quarter_recv.at[z], {"width": targets[h]},
        )
        for h in both_halves
    ]
    image, image_in, quarter_in, final = {}, {}, {}, {}
    plane, plane_in, share, term_out, hop, hop_in = {}, {}, {}, {}, {}, {}
    for k in range(1, m):
        f = slabs[k]
        quarter_in[k] = arriving(text_all.at[0, f], quarter_recv.at[f])
        for p in both_halves:
            mine, theirs = image_all.at[z, :, spans[p]], image_all.at[f, :, spans[p]]
            image[p, k] = remote(
                mine, mine, image_send.at[p, k], image_recv.at[p, z], {"width": f}
            )
            image_in[p, k] = arriving(theirs, image_recv.at[p, f])
    relay, near_out, outer_out, inner_out, back_in = [], [], [], [], []
    for p in both_halves:
        passed = image_all.at[far_outer, :, spans[p]]
        relay.append(
            remote(
                passed, passed, relay_send.at[p], image_recv.at[p, far_outer], {"width": partner}
            )
        )

        def back(i, slot, device):
            return remote(
                image_terms.at[p, i], image_got.at[p, slot],
                back_send.at[p, i], back_recv.at[p, slot], {"width": device},
            )

        near_out.append(back(2, 2, partner))
        outer_out.append([back(0, 0, partner), back(1, 1, partner)])
        inner_out.append([back(0, 3, far_outer), back(1, 3, far_inner)])
        back_in.append([arriving(image_got.at[p, i], back_recv.at[p, i]) for i in range(4)])
    final_in = [arriving(text_final.at[h], final_recv.at[h]) for h in both_halves]
    for r in range(chips):
        for k in range(m):
            f = slabs[k]
            plane_in[r, k] = arriving(text_all.at[r, f], plane_recv.at[r, f])
            share[r, k] = remote(
                text_all.at[r, f], text_all.at[r, f], share_send.at[r, k], plane_recv.at[r, f],
                {"tour": sibling},
            )
            if r > 0:
                plane[r, k] = remote(
                    text_all.at[0, f], text_all.at[chips - r, f],
                    plane_send.at[r, k], plane_recv.at[chips - r, f], {"tour": keepers[r]},
                )
    for i in range(m):
        term_out[i] = remote(
            text_terms.at[i], term_got.at[i], term_send.at[i], term_recv.at[i], {"tour": sibling}
        )
        for r in range(1, chips):
            hop[i, r] = remote(
                text_terms.at[i, r], text_got.at[i, chips - r - 1],
                hop_send.at[i, r], hop_recv.at[i, chips - r], {"tour": keepers[r]},
            )
            hop_in[i, r] = arriving(text_got.at[i, r - 1], hop_recv.at[i, r])
        if i < m - 1:
            final[i] = remote(
                text_sums.at[i], text_final.at[plane_half],
                final_send.at[i], final_recv.at[plane_half], {"width": order[i]},
            )

    barrier = pltpu.get_barrier_semaphore()
    for k in range(1, m):
        pl.semaphore_signal(barrier, inc=1, device_id={"width": slabs[k]}, device_id_type=MESH)
    for k in range(1, n):
        pl.semaphore_signal(
            barrier, inc=1, device_id={"tour": lax.rem(t + k, n)}, device_id_type=MESH
        )
    for load in loads:
        load.wait()
    for h in both_halves:
        @pl.when(targets[h] == z)
        def _():
            text_all[0, z] = texts[:, spans[h]]
    pl.semaphore_wait(barrier, n + m - 2)

    for h in both_halves:
        @pl.when(elsewhere[h])
        def _():
            quarter[h].start()
    for p in both_halves:
        for k in (2, 1, 3):
            @pl.when(direct[k])
            def _():
                image[p, k].start()

    def pass_on(p):
        @pl.when(inner)
        def _():
            image_in[p, 2].wait_recv()
            relay[p].start()

    @pl.when(keeper)
    def _():
        for k in range(m):
            if k > 0:
                quarter_in[k].wait_recv()
            for r in range(1, chips):
                plane[r, k].start()
            share[0, k].start()

    spot = jnp.broadcast_to(matches[...].astype(jnp.float32), (half, rows)).T
    pass_on(0)

    @pl.when(keeper)
    def _():
        for k in range(m):
            for r in range(1, chips):
                plane_in[r, k].wait_recv()
                share[r, k].start()

    @pl.when(helper)
    def _():
        for k in range(m):
            for r in range(chips):
                plane_in[r, k].wait_recv()

    def text_slab(f):
        return jnp.concatenate([text_all[r, f] for r in range(chips)], axis=1)

    column = lax.broadcasted_iota(jnp.int32, (half, half), 1) + plane_half * half
    column = column.astype(jnp.float32)
    kept_label = jnp.where(keeper, 1.0, 0.0)
    counts = [len([s for s in range(-REACH, REACH + 1) if s % n == d]) for d in range(n)]
    times = []
    for r in range(chips):
        distance = lax.rem(t - keepers[r] + n, n)
        count = jnp.float32(0)
        for d in range(n):
            count = jnp.where(distance == d, jnp.float32(counts[d]), count)
        times.append(count)

    weights = []
    for p in both_halves:
        total = None
        for k in range(m):
            if k == 2:
                @pl.when(outer)
                def _():
                    image_in[p, 2].wait_recv()
            elif k > 0:
                image_in[p, k].wait_recv()
            term = cross_cols(image_all[slabs[k], :, spans[p]], text_slab(slabs[k]))
            total = term if total is None else total + term
        probs = jax.nn.sigmoid(temper * total + offset_bias)
        pieces = []
        for r in range(chips):
            piece = probs[:, r * half : (r + 1) * half]
            if r == 0:
                piece = piece - kept_label * (column == spot[spans[p]]).astype(jnp.float32)
            pieces.append(piece.astype(jnp.bfloat16).astype(jnp.float32) * times[r])
        pieces = jnp.concatenate(pieces, axis=1)
        weights.append(pieces.astype(jnp.bfloat16))
        turned = pieces.T.astype(jnp.bfloat16)

        for i, f in enumerate(order):
            term = jnp.dot(text_slab(f), turned, preferred_element_type=jnp.float32)
            if i < 2:
                @pl.when(outer)
                def _():
                    image_terms[p, i] = term.astype(jnp.bfloat16)
                    outer_out[p][i].start()

                @pl.when(inner)
                def _():
                    image_sums[p, i] = term
            elif i == 2:
                image_terms[p, 2] = term.astype(jnp.bfloat16)
                near_out[p].start()
            else:
                image_final[:, spans[p]] = term
        if p == 0:
            pass_on(1)
    weights = jnp.concatenate(weights, axis=0)

    def combine(p):
        @pl.when(inner)
        def _():
            for i in range(2):
                back_in[p][i].wait_recv()
                value = image_sums[p, i] + image_got[p, i].astype(jnp.float32)
                image_terms[p, i] = value.astype(jnp.bfloat16)
                inner_out[p][i].start()

    combine(0)
    for i, f in enumerate(order):
        term = jnp.dot(image_all[f], weights, preferred_element_type=jnp.float32)
        terms = [term[:, r * half : (r + 1) * half] for r in range(chips)]

        @pl.when(helper)
        def _():
            for r in range(chips):
                text_terms[i, r] = terms[r].astype(jnp.bfloat16)
            term_out[i].start()

        @pl.when(keeper)
        def _():
            term_out[i].wait_recv()
            for r in range(1, chips):
                both = terms[r] + term_got[i, r].astype(jnp.float32)
                text_terms[i, r] = both.astype(jnp.bfloat16)
                hop[i, r].start()
            text_own[i] = terms[0] + term_got[i, 0].astype(jnp.float32)

    combine(1)

    @pl.when(keeper)
    def _():
        for i in range(m):
            value = text_own[i]
            for r in range(1, chips):
                hop_in[i, r].wait_recv()
                value = value + text_got[i, r - 1].astype(jnp.float32)
            if i == m - 1:
                text_final[plane_half] = value
            else:
                text_sums[i] = value
                final[i].start()

    stores = []
    for p in both_halves:
        value = image_final[:, spans[p]]
        for i in (2, 3):
            back_in[p][i].wait_recv()
            value = value + image_got[p, i].astype(jnp.float32)
        image_final[:, spans[p]] = value
        stores.append(
            pltpu.make_async_copy(
                image_final.at[:, spans[p]], grad_image.at[:, spans[p]], store_sem.at[p]
            )
        )
        stores[-1].start()
    for h in both_halves:
        @pl.when(elsewhere[h])
        def _():
            final_in[h].wait_recv()
            quarter[h].wait_send()
        stores.append(
            pltpu.make_async_copy(
                text_final.at[h], grad_text.at[:, spans[h]], store_sem.at[halves + h]
            )
        )
        stores[-1].start()
    for p in both_halves:
        for k in range(1, m):
            @pl.when(direct[k])
            def _():
                image[p, k].wait_send()
        near_out[p].wait_send()

        @pl.when(outer)
        def _():
            for copy in outer_out[p]:
                copy.wait_send()

        @pl.when(inner)
        def _():
            for copy in [relay[p]] + inner_out[p]:
                copy.wait_send()

    @pl.when(keeper)
    def _():
        for group in (plane, share, hop, final):
            for copy in group.values():
                copy.wait_send()

    @pl.when(helper)
    def _():
        for copy in term_out.values():
            copy.wait_send()

    for store in stores:
        store.wait()


def whole(images, texts, matches, scale, shift_bias):
    n, m = lax.axis_size("tour"), lax.axis_size("width")
    rows, width = images.shape
    chips, halves = n // 2, m // 2
    half = rows // halves
    hbm = pl.BlockSpec(memory_space=pltpu.HBM)
    smem = pl.BlockSpec(memory_space=pltpu.SMEM)
    out = jax.ShapeDtypeStruct((width, rows), jnp.float32)

    def dma(*shape):
        return pltpu.SemaphoreType.DMA(shape)

    def narrow(*shape):
        return pltpu.VMEM(shape, jnp.bfloat16)

    def wide(*shape):
        return pltpu.VMEM(shape, jnp.float32)

    grads = pl.pallas_call(
        functools.partial(kernel, n, m),
        out_shape=(out, out),
        in_specs=[hbm, hbm, hbm, smem, smem],
        out_specs=(hbm, hbm),
        scratch_shapes=[
            narrow(width, rows), pltpu.VMEM((1, rows), jnp.int32), narrow(m, width, rows),
            narrow(chips, m, width, half), narrow(m, chips, width, half),
            narrow(m, chips, width, half), narrow(m, chips - 1, width, half),
            wide(m, width, half), wide(m - 1, width, half), wide(halves, width, half),
            narrow(halves, 3, width, half), wide(halves, 2, width, half),
            narrow(halves, 4, width, half), wide(width, rows),
            dma(3), dma(2 * halves), dma(halves), dma(halves), dma(m), dma(halves, m), dma(halves, m),
            dma(chips, m), dma(chips, m), dma(chips, m), dma(m), dma(m), dma(m, chips), dma(m, chips),
            dma(halves, 3), dma(halves, 4), dma(m), dma(halves),
        ],
        compiler_params=pltpu.CompilerParams(
            collective_id=0, has_side_effects=True, vmem_limit_bytes=60 * 1024 * 1024
        ),
    )(images.T, texts.T, matches, scale, shift_bias)
    return tuple(scale[0] * grad.T for grad in grads)


def solution(mesh):
    placed = (P("tour", "width"), P("tour", "width"), P("tour", None), P(), P())
    n, m = mesh.shape["tour"], mesh.shape["width"]
    body = whole if n <= 2 * REACH + 1 and n % 2 == 0 and m == 4 else band
    return jax.shard_map(
        body,
        mesh=mesh,
        in_specs=placed,
        out_specs=(P("tour", "width"), P("tour", "width")),
        check_vma=False,
    )
```

```python
import functools

import jax
import jax.numpy as jnp
from jax import lax
from jax.experimental import pallas as pl
from jax.experimental.pallas import tpu as pltpu
from jax.sharding import PartitionSpec as P

REACH = 7
MESH = pl.DeviceIdType.MESH


def shifted(block, axis, distance):
    devices = range(lax.axis_size(axis))
    route = [((i - distance) % len(devices), i) for i in devices]
    return lax.ppermute(block, axis, route)


def cross_rows(left, right):
    return lax.dot_general(
        left, right, (((1,), (1,)), ((), ())), preferred_element_type=jnp.float32
    )


def cross_cols(weights, right):
    return lax.dot_general(
        weights, right, (((0,), (0,)), ((), ())), preferred_element_type=jnp.float32
    )


def band(images, texts, matches, scale, shift_bias):
    temper = scale[0]
    offset_bias = shift_bias[0]
    rows = images.shape[0]
    columns = lax.broadcasted_iota(jnp.int32, (rows, rows), 1)
    positive = (columns == matches[0][:, None]).astype(jnp.float32)

    def to_weights(total, label):
        probs = jax.nn.sigmoid(temper * total + offset_bias)
        if label is not None:
            probs = probs - label
        return probs.astype(jnp.bfloat16)

    def finish(parts, labels):
        totals = lax.psum(parts, "width")
        return tuple((to_weights(total, label) for total, label in zip(totals, labels)))

    own = finish((cross_rows(images, texts),), (positive,))[0]
    grad_image = jnp.dot(own, texts, preferred_element_type=jnp.float32)
    grad_text = cross_cols(own, images)
    for step in range(1, REACH + 1):
        lower = shifted(texts, "tour", step)
        upper = shifted(texts, "tour", -step)
        weight_low, weight_up = finish(
            (cross_rows(images, lower), cross_rows(images, upper)), (None, None)
        )
        grad_image = grad_image + jnp.dot(weight_low, lower, preferred_element_type=jnp.float32)
        grad_image = grad_image + jnp.dot(weight_up, upper, preferred_element_type=jnp.float32)
        back_low = shifted(cross_cols(weight_low, images), "tour", -step)
        back_up = shifted(cross_cols(weight_up, images), "tour", step)
        grad_text = grad_text + back_low + back_up
    return (temper * grad_image, temper * grad_text)


def kernel(
    n, m, images_in, texts_in, matches_in, scale, shift_bias, grad_image, grad_text,
    texts, matches, image_all, text_all, text_terms, term_got, hop_terms, text_got, text_own, text_sums, text_final,
    image_terms, image_sums, image_got, image_final,
    load_sem, store_sem, relay_send, quarter_send, quarter_recv, image_send, image_recv,
    plane_send, plane_recv, share_send, term_send, term_recv, hop_send, hop_recv,
    back_send, back_recv, final_send, final_recv,
):
    t, z = lax.axis_index("tour"), lax.axis_index("width")
    width, rows = texts.shape
    cores = 2
    halves, chips = m // cores, n // cores
    half = rows // halves
    temper, offset_bias = scale[0], shift_bias[0]
    core, chip = lax.rem(t, cores), lax.div(t, cores)
    plane_core, plane_half = lax.div(z, halves), lax.rem(z, halves)
    sibling = chip * cores + (cores - 1 - core)
    slabs = [lax.rem(z + k, m) for k in range(m)]
    keepers = [lax.rem(chip + r, chips) * cores + plane_core for r in range(chips)]
    peers = [lax.rem(chip + r, chips) * cores + core for r in range(chips)]
    targets = [core * halves + h for h in range(halves)]
    same_core = lax.rem(z, cores) == core
    local = [jnp.logical_and(target == z, same_core) for target in targets]
    elsewhere = [jnp.logical_not(here) for here in local]
    landing, origin = chip * cores + lax.rem(z, cores), chip * cores + plane_core
    both_halves = range(halves)
    spans = [slice(p * half, (p + 1) * half) for p in both_halves]
    outer = jnp.logical_or(z == 0, z == m - 1)
    inner = jnp.logical_not(outer)
    low = z < halves
    partner = jnp.where(low, 1 - z, 2 * m - 3 - z)
    far_inner = jnp.where(low, halves, halves - 1)
    far_outer = jnp.where(low, m - 1, 0)
    direct = [jnp.logical_or(inner, f != far_outer) for f in slabs]
    order = (far_outer, far_inner, partner, z)
    far_start = jnp.where(low, halves, 0)
    mine = [far_start + core, halves - far_start + core]
    theirs = [far_start + cores - 1 - core, halves - far_start + cores - 1 - core]
    home = [jnp.logical_and(f == z, plane_core == core) for f in mine]
    abroad = [jnp.logical_not(here) for here in home]

    loads = [
        pltpu.make_async_copy(images_in, image_all.at[z], load_sem.at[0]),
        pltpu.make_async_copy(texts_in, texts, load_sem.at[1]),
        pltpu.make_async_copy(matches_in, matches, load_sem.at[2]),
    ]
    for load in loads:
        load.start()

    def remote(src, dst, send_sem, recv_sem, device):
        return pltpu.make_async_remote_copy(
            src_ref=src, dst_ref=dst, send_sem=send_sem, recv_sem=recv_sem,
            device_id=device, device_id_type=MESH,
        )

    def arriving(dst, recv_sem):
        return remote(dst, dst, quarter_send.at[0], recv_sem, {"width": slabs[1]})

    quarter = [
        remote(
            texts.at[:, spans[h]], text_all.at[0, z],
            quarter_send.at[h], quarter_recv.at[z], {"tour": landing, "width": targets[h]},
        )
        for h in both_halves
    ]
    image, image_in, quarter_in, final = {}, {}, {}, {}
    plane, plane_in, share, share_in, term_out, hop, hop_in = {}, {}, {}, {}, {}, {}, {}
    for k in range(1, m):
        f = slabs[k]
        for p in both_halves:
            sent, comes = image_all.at[z, :, spans[p]], image_all.at[f, :, spans[p]]
            image[p, k] = remote(
                sent, sent, image_send.at[p, k], image_recv.at[p, z], {"width": f}
            )
            image_in[p, k] = arriving(comes, image_recv.at[p, f])
    relay, near_out, outer_out, inner_out, back_in = [], [], [], [], []
    for p in both_halves:
        passed = image_all.at[far_outer, :, spans[p]]
        relay.append(
            remote(
                passed, passed, relay_send.at[p], image_recv.at[p, far_outer], {"width": partner}
            )
        )

        def back(i, slot, device):
            return remote(
                image_terms.at[p, i], image_got.at[p, slot],
                back_send.at[p, i], back_recv.at[p, slot], {"width": device},
            )

        near_out.append(back(2, 2, partner))
        outer_out.append([back(0, 0, partner), back(1, 1, partner)])
        inner_out.append([back(0, 3, far_outer), back(1, 3, far_inner)])
        back_in.append([arriving(image_got.at[p, i], back_recv.at[p, i]) for i in range(4)])
    final_in = [arriving(text_final.at[h], final_recv.at[h]) for h in both_halves]
    for j in range(2):
        f, g = mine[j], theirs[j]
        quarter_in[j] = arriving(text_all.at[0, f], quarter_recv.at[f])
        term_out[j] = remote(
            text_terms.at[j], term_got.at[j], term_send.at[j], term_recv.at[j], {"tour": sibling}
        )
        final[j] = remote(
            text_sums.at[j], text_final.at[plane_half], final_send.at[j], final_recv.at[plane_half],
            {"tour": origin, "width": f},
        )
        for r in range(chips):
            plane_in[r, j] = arriving(text_all.at[r, f], plane_recv.at[r, f])
            share_in[r, j] = arriving(text_all.at[r, g], plane_recv.at[r, g])
            share[r, j] = remote(
                text_all.at[r, f], text_all.at[r, f], share_send.at[r, j], plane_recv.at[r, f],
                {"tour": sibling},
            )
            if r > 0:
                plane[r, j] = remote(
                    text_all.at[0, f], text_all.at[chips - r, f],
                    plane_send.at[r, j], plane_recv.at[chips - r, f], {"tour": peers[r]},
                )
                hop[r, j] = remote(
                    hop_terms.at[j, r - 1], text_got.at[j, chips - r - 1],
                    hop_send.at[r, j], hop_recv.at[chips - r, j], {"tour": peers[r]},
                )
                hop_in[r, j] = arriving(text_got.at[j, r - 1], hop_recv.at[r, j])

    barrier = pltpu.get_barrier_semaphore()
    for k in range(1, m):
        pl.semaphore_signal(barrier, inc=1, device_id={"width": slabs[k]}, device_id_type=MESH)
        pl.semaphore_signal(
            barrier, inc=1, device_id={"tour": sibling, "width": slabs[k]}, device_id_type=MESH
        )
    for other in peers[1:] + [sibling]:
        pl.semaphore_signal(barrier, inc=1, device_id={"tour": other}, device_id_type=MESH)
    for load in loads:
        load.wait()
    for h in both_halves:
        @pl.when(local[h])
        def _():
            text_all[0, z] = texts[:, spans[h]]
    pl.semaphore_wait(barrier, 2 * (m - 1) + chips)

    for h in both_halves:
        @pl.when(elsewhere[h])
        def _():
            quarter[h].start()
    for p in both_halves:
        for k in (2, 1, 3):
            @pl.when(direct[k])
            def _():
                image[p, k].start()

    def pass_on(p):
        @pl.when(inner)
        def _():
            image_in[p, 2].wait_recv()
            relay[p].start()

    for j in (1, 0):
        @pl.when(abroad[j])
        def _():
            quarter_in[j].wait_recv()
        for r in range(1, chips):
            plane[r, j].start()
        share[0, j].start()

    spot = jnp.broadcast_to(matches[...].astype(jnp.float32), (half, rows)).T
    pass_on(0)

    for j in (1, 0):
        for r in range(1, chips):
            plane_in[r, j].wait_recv()
            share[r, j].start()
    for j in (1, 0):
        for r in range(chips):
            share_in[r, j].wait_recv()

    def text_slab(f):
        return jnp.concatenate([text_all[r, f] for r in range(chips)], axis=1)

    column = lax.broadcasted_iota(jnp.int32, (half, half), 1) + plane_half * half
    column = column.astype(jnp.float32)
    kept_label = jnp.where(core == plane_core, 1.0, 0.0)
    counts = [len([s for s in range(-REACH, REACH + 1) if s % n == d]) for d in range(n)]
    times = []
    for r in range(chips):
        distance = lax.rem(t - keepers[r] + n, n)
        count = jnp.float32(0)
        for d in range(n):
            count = jnp.where(distance == d, jnp.float32(counts[d]), count)
        times.append(count)

    weights = []
    for p in both_halves:
        total = None
        for k in range(m):
            if k == 2:
                @pl.when(outer)
                def _():
                    image_in[p, 2].wait_recv()
            elif k > 0:
                image_in[p, k].wait_recv()
            term = cross_cols(image_all[slabs[k], :, spans[p]], text_slab(slabs[k]))
            total = term if total is None else total + term
        probs = jax.nn.sigmoid(temper * total + offset_bias)
        pieces = []
        for r in range(chips):
            piece = probs[:, r * half : (r + 1) * half]
            if r == 0:
                piece = piece - kept_label * (column == spot[spans[p]]).astype(jnp.float32)
            pieces.append(piece.astype(jnp.bfloat16).astype(jnp.float32) * times[r])
        pieces = jnp.concatenate(pieces, axis=1)
        weights.append(pieces.astype(jnp.bfloat16))
        turned = pieces.T.astype(jnp.bfloat16)

        for i, f in enumerate(order):
            term = jnp.dot(text_slab(f), turned, preferred_element_type=jnp.float32)
            if i < 2:
                @pl.when(outer)
                def _():
                    image_terms[p, i] = term.astype(jnp.bfloat16)
                    outer_out[p][i].start()

                @pl.when(inner)
                def _():
                    image_sums[p, i] = term
            elif i == 2:
                image_terms[p, 2] = term.astype(jnp.bfloat16)
                near_out[p].start()
            else:
                image_final[:, spans[p]] = term
        if p == 0:
            pass_on(1)
    weights = jnp.concatenate(weights, axis=0)

    def combine(p):
        @pl.when(inner)
        def _():
            for i in range(2):
                back_in[p][i].wait_recv()
                value = image_sums[p, i] + image_got[p, i].astype(jnp.float32)
                image_terms[p, i] = value.astype(jnp.bfloat16)
                inner_out[p][i].start()

    combine(0)

    def text_term(f):
        term = jnp.dot(image_all[f], weights, preferred_element_type=jnp.float32)
        return [term[:, r * half : (r + 1) * half] for r in range(chips)]

    for j in range(2):
        terms = text_term(theirs[j])
        for r in range(chips):
            text_terms[j, r] = terms[r].astype(jnp.bfloat16)
        term_out[j].start()
    for j in range(2):
        terms = text_term(mine[j])
        term_out[j].wait_recv()
        for r in range(1, chips):
            both = terms[r] + term_got[j, r].astype(jnp.float32)
            hop_terms[j, r - 1] = both.astype(jnp.bfloat16)
            hop[r, j].start()
        text_own[j] = terms[0] + term_got[j, 0].astype(jnp.float32)

    combine(1)
    for j in range(2):
        value = text_own[j]
        for r in range(1, chips):
            hop_in[r, j].wait_recv()
            value = value + text_got[j, r - 1].astype(jnp.float32)
        text_sums[j] = value

        @pl.when(home[j])
        def _():
            text_final[plane_half] = text_sums[j]

        @pl.when(abroad[j])
        def _():
            final[j].start()

    stores = []
    for p in both_halves:
        value = image_final[:, spans[p]]
        for i in (2, 3):
            back_in[p][i].wait_recv()
            value = value + image_got[p, i].astype(jnp.float32)
        image_final[:, spans[p]] = value
        stores.append(
            pltpu.make_async_copy(
                image_final.at[:, spans[p]], grad_image.at[:, spans[p]], store_sem.at[p]
            )
        )
        stores[-1].start()
    for h in both_halves:
        @pl.when(elsewhere[h])
        def _():
            final_in[h].wait_recv()
            quarter[h].wait_send()
        stores.append(
            pltpu.make_async_copy(
                text_final.at[h], grad_text.at[:, spans[h]], store_sem.at[halves + h]
            )
        )
        stores[-1].start()
    for p in both_halves:
        for k in range(1, m):
            @pl.when(direct[k])
            def _():
                image[p, k].wait_send()
        near_out[p].wait_send()

        @pl.when(outer)
        def _():
            for copy in outer_out[p]:
                copy.wait_send()

        @pl.when(inner)
        def _():
            for copy in [relay[p]] + inner_out[p]:
                copy.wait_send()

    for group in (plane, share, hop, term_out):
        for copy in group.values():
            copy.wait_send()
    for j in range(2):
        @pl.when(abroad[j])
        def _():
            final[j].wait_send()

    for store in stores:
        store.wait()


def whole(images, texts, matches, scale, shift_bias):
    n, m = lax.axis_size("tour"), lax.axis_size("width")
    rows, width = images.shape
    chips, halves = n // 2, m // 2
    half = rows // halves
    hbm = pl.BlockSpec(memory_space=pltpu.HBM)
    smem = pl.BlockSpec(memory_space=pltpu.SMEM)
    out = jax.ShapeDtypeStruct((width, rows), jnp.float32)

    def dma(*shape):
        return pltpu.SemaphoreType.DMA(shape)

    def narrow(*shape):
        return pltpu.VMEM(shape, jnp.bfloat16)

    def wide(*shape):
        return pltpu.VMEM(shape, jnp.float32)

    grads = pl.pallas_call(
        functools.partial(kernel, n, m),
        out_shape=(out, out),
        in_specs=[hbm, hbm, hbm, smem, smem],
        out_specs=(hbm, hbm),
        scratch_shapes=[
            narrow(width, rows), pltpu.VMEM((1, rows), jnp.int32), narrow(m, width, rows),
            narrow(chips, m, width, half), narrow(2, chips, width, half),
            narrow(2, chips, width, half), narrow(2, chips - 1, width, half),
            narrow(2, chips - 1, width, half),
            wide(2, width, half), wide(2, width, half), wide(halves, width, half),
            narrow(halves, 3, width, half), wide(halves, 2, width, half),
            narrow(halves, 4, width, half), wide(width, rows),
            dma(3), dma(2 * halves), dma(halves), dma(halves), dma(m), dma(halves, m), dma(halves, m),
            dma(chips, 2), dma(chips, m), dma(chips, 2), dma(2), dma(2), dma(chips, 2), dma(chips, 2),
            dma(halves, 3), dma(halves, 4), dma(2), dma(halves),
        ],
        compiler_params=pltpu.CompilerParams(
            collective_id=0, has_side_effects=True, vmem_limit_bytes=60 * 1024 * 1024
        ),
    )(images.T, texts.T, matches, scale, shift_bias)
    return tuple(scale[0] * grad.T for grad in grads)


def solution(mesh):
    placed = (P("tour", "width"), P("tour", "width"), P("tour", None), P(), P())
    n, m = mesh.shape["tour"], mesh.shape["width"]
    body = whole if n <= 2 * REACH + 1 and n % 2 == 0 and m == 4 else band
    return jax.shard_map(
        body,
        mesh=mesh,
        in_specs=placed,
        out_specs=(P("tour", "width"), P("tour", "width")),
        check_vma=False,
    )
```

```python
import functools

import jax
import jax.numpy as jnp
from jax import lax
from jax.experimental import pallas as pl
from jax.experimental.pallas import tpu as pltpu
from jax.sharding import PartitionSpec as P

REACH = 7
MESH = pl.DeviceIdType.MESH


def shifted(block, axis, distance):
    devices = range(lax.axis_size(axis))
    route = [((i - distance) % len(devices), i) for i in devices]
    return lax.ppermute(block, axis, route)


def cross_rows(left, right):
    return lax.dot_general(
        left, right, (((1,), (1,)), ((), ())), preferred_element_type=jnp.float32
    )


def cross_cols(weights, right):
    return lax.dot_general(
        weights, right, (((0,), (0,)), ((), ())), preferred_element_type=jnp.float32
    )


def band(images, texts, matches, scale, shift_bias):
    temper = scale[0]
    offset_bias = shift_bias[0]
    rows = images.shape[0]
    columns = lax.broadcasted_iota(jnp.int32, (rows, rows), 1)
    positive = (columns == matches[0][:, None]).astype(jnp.float32)

    def to_weights(total, label):
        probs = jax.nn.sigmoid(temper * total + offset_bias)
        if label is not None:
            probs = probs - label
        return probs.astype(jnp.bfloat16)

    def finish(parts, labels):
        totals = lax.psum(parts, "width")
        return tuple((to_weights(total, label) for total, label in zip(totals, labels)))

    own = finish((cross_rows(images, texts),), (positive,))[0]
    grad_image = jnp.dot(own, texts, preferred_element_type=jnp.float32)
    grad_text = cross_cols(own, images)
    for step in range(1, REACH + 1):
        lower = shifted(texts, "tour", step)
        upper = shifted(texts, "tour", -step)
        weight_low, weight_up = finish(
            (cross_rows(images, lower), cross_rows(images, upper)), (None, None)
        )
        grad_image = grad_image + jnp.dot(weight_low, lower, preferred_element_type=jnp.float32)
        grad_image = grad_image + jnp.dot(weight_up, upper, preferred_element_type=jnp.float32)
        back_low = shifted(cross_cols(weight_low, images), "tour", -step)
        back_up = shifted(cross_cols(weight_up, images), "tour", step)
        grad_text = grad_text + back_low + back_up
    return (temper * grad_image, temper * grad_text)


def kernel(
    n, m, images_in, texts_in, matches_in, scale, shift_bias, grad_image, grad_text,
    texts, matches, image_all, text_all, text_terms, term_got, hop_terms, text_got, text_own, text_sums, text_final,
    image_terms, image_sums, image_got, image_final,
    load_sem, store_sem, relay_send, quarter_send, quarter_recv, image_send, image_recv,
    plane_send, plane_recv, share_send, term_send, term_recv, hop_send, hop_recv,
    back_send, back_recv, final_send, final_recv,
):
    t, z = lax.axis_index("tour"), lax.axis_index("width")
    width, rows = images_in.shape
    cores = 2
    halves, chips = m // cores, n // cores
    half = rows // halves
    temper, offset_bias = scale[0], shift_bias[0]
    core, chip = lax.rem(t, cores), lax.div(t, cores)
    plane_core, plane_half = lax.div(z, halves), lax.rem(z, halves)
    sibling = chip * cores + (cores - 1 - core)
    slabs = [lax.rem(z + k, m) for k in range(m)]
    keepers = [lax.rem(chip + r, chips) * cores + plane_core for r in range(chips)]
    peers = [lax.rem(chip + r, chips) * cores + core for r in range(chips)]
    targets = [core * halves + h for h in range(halves)]
    same_core = lax.rem(z, cores) == core
    local = [jnp.logical_and(target == z, same_core) for target in targets]
    elsewhere = [jnp.logical_not(here) for here in local]
    landing, origin = chip * cores + lax.rem(z, cores), chip * cores + plane_core
    both_halves = range(halves)
    spans = [slice(p * half, (p + 1) * half) for p in both_halves]
    outer = jnp.logical_or(z == 0, z == m - 1)
    inner = jnp.logical_not(outer)
    low = z < halves
    partner = jnp.where(low, 1 - z, 2 * m - 3 - z)
    far_inner = jnp.where(low, halves, halves - 1)
    far_outer = jnp.where(low, m - 1, 0)
    direct = [jnp.logical_or(inner, f != far_outer) for f in slabs]
    order = (far_outer, far_inner, partner, z)
    far_start = jnp.where(low, halves, 0)
    mine = [far_start + core, halves - far_start + core]
    theirs = [far_start + cores - 1 - core, halves - far_start + cores - 1 - core]
    home = [jnp.logical_and(f == z, plane_core == core) for f in mine]
    abroad = [jnp.logical_not(here) for here in home]

    loads = [pltpu.make_async_copy(matches_in, matches, load_sem.at[2 * halves])]
    for p in both_halves:
        loads += [
            pltpu.make_async_copy(texts_in.at[:, spans[p]], texts.at[p], load_sem.at[halves + p]),
            pltpu.make_async_copy(images_in.at[:, spans[p]], image_all.at[z, p], load_sem.at[p]),
        ]
    for load in loads:
        load.start()

    def remote(src, dst, send_sem, recv_sem, device):
        return pltpu.make_async_remote_copy(
            src_ref=src, dst_ref=dst, send_sem=send_sem, recv_sem=recv_sem,
            device_id=device, device_id_type=MESH,
        )

    def arriving(dst, recv_sem):
        return remote(dst, dst, quarter_send.at[0], recv_sem, {"width": slabs[1]})

    quarter = [
        remote(
            texts.at[h], text_all.at[0, z],
            quarter_send.at[h], quarter_recv.at[z], {"tour": landing, "width": targets[h]},
        )
        for h in both_halves
    ]
    image, image_in, quarter_in, final = {}, {}, {}, {}
    plane, plane_in, share, share_in, term_out, hop, hop_in = {}, {}, {}, {}, {}, {}, {}
    for k in range(1, m):
        f = slabs[k]
        for p in both_halves:
            sent, comes = image_all.at[z, p], image_all.at[f, p]
            image[p, k] = remote(
                sent, sent, image_send.at[p, k], image_recv.at[p, z], {"width": f}
            )
            image_in[p, k] = arriving(comes, image_recv.at[p, f])
    relay, near_out, outer_out, inner_out, back_in = [], [], [], [], []
    for p in both_halves:
        passed = image_all.at[far_outer, p]
        relay.append(
            remote(
                passed, passed, relay_send.at[p], image_recv.at[p, far_outer], {"width": partner}
            )
        )

        def back(i, slot, device):
            return remote(
                image_terms.at[p, i], image_got.at[p, slot],
                back_send.at[p, i], back_recv.at[p, slot], {"width": device},
            )

        near_out.append(back(2, 2, partner))
        outer_out.append([back(0, 0, partner), back(1, 1, partner)])
        inner_out.append([back(0, 3, far_outer), back(1, 3, far_inner)])
        back_in.append([arriving(image_got.at[p, i], back_recv.at[p, i]) for i in range(4)])
    final_in = [arriving(text_final.at[h], final_recv.at[h]) for h in both_halves]
    for j in range(2):
        f, g = mine[j], theirs[j]
        quarter_in[j] = arriving(text_all.at[0, f], quarter_recv.at[f])
        term_out[j] = remote(
            text_terms.at[j], term_got.at[j], term_send.at[j], term_recv.at[j], {"tour": sibling}
        )
        final[j] = remote(
            text_sums.at[j], text_final.at[plane_half], final_send.at[j], final_recv.at[plane_half],
            {"tour": origin, "width": f},
        )
        for r in range(chips):
            plane_in[r, j] = arriving(text_all.at[r, f], plane_recv.at[r, f])
            share_in[r, j] = arriving(text_all.at[r, g], plane_recv.at[r, g])
            share[r, j] = remote(
                text_all.at[r, f], text_all.at[r, f], share_send.at[r, j], plane_recv.at[r, f],
                {"tour": sibling},
            )
            if r > 0:
                plane[r, j] = remote(
                    text_all.at[0, f], text_all.at[chips - r, f],
                    plane_send.at[r, j], plane_recv.at[chips - r, f], {"tour": peers[r]},
                )
                hop[r, j] = remote(
                    hop_terms.at[j, r - 1], text_got.at[j, chips - r - 1],
                    hop_send.at[r, j], hop_recv.at[chips - r, j], {"tour": peers[r]},
                )
                hop_in[r, j] = arriving(text_got.at[j, r - 1], hop_recv.at[r, j])

    barrier = pltpu.get_barrier_semaphore()
    for k in range(1, m):
        pl.semaphore_signal(barrier, inc=1, device_id={"width": slabs[k]}, device_id_type=MESH)
        pl.semaphore_signal(
            barrier, inc=1, device_id={"tour": sibling, "width": slabs[k]}, device_id_type=MESH
        )
    for other in peers[1:] + [sibling]:
        pl.semaphore_signal(barrier, inc=1, device_id={"tour": other}, device_id_type=MESH)
    for load in loads:
        load.wait()
    for h in both_halves:
        @pl.when(local[h])
        def _():
            text_all[0, z] = texts[h]
    pl.semaphore_wait(barrier, 2 * (m - 1) + chips)

    for h in both_halves:
        @pl.when(elsewhere[h])
        def _():
            quarter[h].start()

    def send_images(p):
        for k in (2, 1, 3):
            @pl.when(direct[k])
            def _():
                image[p, k].start()

    def pass_on(p):
        @pl.when(inner)
        def _():
            image_in[p, 2].wait_recv()
            relay[p].start()

    for j in (1, 0):
        @pl.when(abroad[j])
        def _():
            quarter_in[j].wait_recv()
        for r in range(1, chips):
            plane[r, j].start()
        share[0, j].start()

    send_images(0)
    spot = jnp.broadcast_to(matches[...].astype(jnp.float32), (half, rows)).T
    for k in range(1, m):
        @pl.when(direct[k])
        def _():
            image[0, k].wait_send()
    send_images(1)
    pass_on(0)

    for j in (1, 0):
        for r in range(1, chips):
            plane_in[r, j].wait_recv()
            share[r, j].start()
    for j in (1, 0):
        for r in range(chips):
            share_in[r, j].wait_recv()

    def text_slab(f):
        return jnp.concatenate([text_all[r, f] for r in range(chips)], axis=1)

    column = lax.broadcasted_iota(jnp.int32, (half, half), 1) + plane_half * half
    column = column.astype(jnp.float32)
    kept_label = jnp.where(core == plane_core, 1.0, 0.0)
    counts = [len([s for s in range(-REACH, REACH + 1) if s % n == d]) for d in range(n)]
    times = []
    for r in range(chips):
        distance = lax.rem(t - keepers[r] + n, n)
        count = jnp.float32(0)
        for d in range(n):
            count = jnp.where(distance == d, jnp.float32(counts[d]), count)
        times.append(count)

    weights = []
    for p in both_halves:
        total = None
        for k in range(m):
            if k == 2:
                @pl.when(outer)
                def _():
                    image_in[p, 2].wait_recv()
            elif k > 0:
                image_in[p, k].wait_recv()
            term = cross_cols(image_all[slabs[k], p], text_slab(slabs[k]))
            total = term if total is None else total + term
        probs = jax.nn.sigmoid(temper * total + offset_bias)
        pieces = []
        for r in range(chips):
            piece = probs[:, r * half : (r + 1) * half]
            if r == 0:
                piece = piece - kept_label * (column == spot[spans[p]]).astype(jnp.float32)
            pieces.append(piece.astype(jnp.bfloat16).astype(jnp.float32) * times[r])
        pieces = jnp.concatenate(pieces, axis=1)
        weights.append(pieces.astype(jnp.bfloat16))
        turned = pieces.T.astype(jnp.bfloat16)

        for i, f in enumerate(order):
            term = jnp.dot(text_slab(f), turned, preferred_element_type=jnp.float32)
            if i < 2:
                @pl.when(outer)
                def _():
                    image_terms[p, i] = term.astype(jnp.bfloat16)
                    outer_out[p][i].start()

                @pl.when(inner)
                def _():
                    image_sums[p, i] = term
            elif i == 2:
                image_terms[p, 2] = term.astype(jnp.bfloat16)
                near_out[p].start()
            else:
                image_final[:, spans[p]] = term
        if p == 0:
            pass_on(1)
    weights = jnp.concatenate(weights, axis=0)

    def combine(p):
        @pl.when(inner)
        def _():
            for i in range(2):
                back_in[p][i].wait_recv()
                value = image_sums[p, i] + image_got[p, i].astype(jnp.float32)
                image_terms[p, i] = value.astype(jnp.bfloat16)
                inner_out[p][i].start()

    def text_term(f):
        slab = jnp.concatenate([image_all[f, p] for p in both_halves], axis=1)
        term = jnp.dot(slab, weights, preferred_element_type=jnp.float32)
        return [term[:, r * half : (r + 1) * half] for r in range(chips)]

    for j in range(2):
        terms = text_term(theirs[j])
        for r in range(chips):
            text_terms[j, r] = terms[r].astype(jnp.bfloat16)
        term_out[j].start()
    combine(0)
    for j in range(2):
        terms = text_term(mine[j])
        term_out[j].wait_recv()
        for r in range(1, chips):
            both = terms[r] + term_got[j, r].astype(jnp.float32)
            hop_terms[j, r - 1] = both.astype(jnp.bfloat16)
            hop[r, j].start()
        text_own[j] = terms[0] + term_got[j, 0].astype(jnp.float32)

    combine(1)
    for j in range(2):
        value = text_own[j]
        for r in range(1, chips):
            hop_in[r, j].wait_recv()
            value = value + text_got[j, r - 1].astype(jnp.float32)
        text_sums[j] = value

        @pl.when(home[j])
        def _():
            text_final[plane_half] = text_sums[j]

        @pl.when(abroad[j])
        def _():
            final[j].start()

    stores = []
    for p in both_halves:
        value = image_final[:, spans[p]]
        for i in (2, 3):
            back_in[p][i].wait_recv()
            value = value + image_got[p, i].astype(jnp.float32)
        image_final[:, spans[p]] = value
        stores.append(
            pltpu.make_async_copy(
                image_final.at[:, spans[p]], grad_image.at[:, spans[p]], store_sem.at[p]
            )
        )
        stores[-1].start()
    for h in both_halves:
        @pl.when(elsewhere[h])
        def _():
            final_in[h].wait_recv()
            quarter[h].wait_send()
        stores.append(
            pltpu.make_async_copy(
                text_final.at[h], grad_text.at[:, spans[h]], store_sem.at[halves + h]
            )
        )
        stores[-1].start()
    for p in both_halves:
        if p == 1:
            for k in range(1, m):
                @pl.when(direct[k])
                def _():
                    image[1, k].wait_send()
        near_out[p].wait_send()

        @pl.when(outer)
        def _():
            for copy in outer_out[p]:
                copy.wait_send()

        @pl.when(inner)
        def _():
            for copy in [relay[p]] + inner_out[p]:
                copy.wait_send()

    for group in (plane, share, hop, term_out):
        for copy in group.values():
            copy.wait_send()
    for j in range(2):
        @pl.when(abroad[j])
        def _():
            final[j].wait_send()

    for store in stores:
        store.wait()


def whole(images, texts, matches, scale, shift_bias):
    n, m = lax.axis_size("tour"), lax.axis_size("width")
    rows, width = images.shape
    chips, halves = n // 2, m // 2
    half = rows // halves
    hbm = pl.BlockSpec(memory_space=pltpu.HBM)
    smem = pl.BlockSpec(memory_space=pltpu.SMEM)
    out = jax.ShapeDtypeStruct((width, rows), jnp.float32)

    def dma(*shape):
        return pltpu.SemaphoreType.DMA(shape)

    def narrow(*shape):
        return pltpu.VMEM(shape, jnp.bfloat16)

    def wide(*shape):
        return pltpu.VMEM(shape, jnp.float32)

    grads = pl.pallas_call(
        functools.partial(kernel, n, m),
        out_shape=(out, out),
        in_specs=[hbm, hbm, hbm, smem, smem],
        out_specs=(hbm, hbm),
        scratch_shapes=[
            narrow(halves, width, half), pltpu.VMEM((1, rows), jnp.int32),
            narrow(m, halves, width, half),
            narrow(chips, m, width, half), narrow(2, chips, width, half),
            narrow(2, chips, width, half), narrow(2, chips - 1, width, half),
            narrow(2, chips - 1, width, half),
            wide(2, width, half), wide(2, width, half), wide(halves, width, half),
            narrow(halves, 3, width, half), wide(halves, 2, width, half),
            narrow(halves, 4, width, half), wide(width, rows),
            dma(2 * halves + 1), dma(2 * halves), dma(halves), dma(halves), dma(m), dma(halves, m), dma(halves, m),
            dma(chips, 2), dma(chips, m), dma(chips, 2), dma(2), dma(2), dma(chips, 2), dma(chips, 2),
            dma(halves, 3), dma(halves, 4), dma(2), dma(halves),
        ],
        compiler_params=pltpu.CompilerParams(
            collective_id=0, has_side_effects=True, vmem_limit_bytes=60 * 1024 * 1024
        ),
    )(images.T, texts.T, matches, scale, shift_bias)
    return tuple(scale[0] * grad.T for grad in grads)


def solution(mesh):
    placed = (P("tour", "width"), P("tour", "width"), P("tour", None), P(), P())
    n, m = mesh.shape["tour"], mesh.shape["width"]
    body = whole if n <= 2 * REACH + 1 and n % 2 == 0 and m == 4 else band
    return jax.shard_map(
        body,
        mesh=mesh,
        in_specs=placed,
        out_specs=(P("tour", "width"), P("tour", "width")),
        check_vma=False,
    )
```

```python
import functools

import jax
import jax.numpy as jnp
from jax import lax
from jax.experimental import pallas as pl
from jax.experimental.pallas import tpu as pltpu
from jax.sharding import PartitionSpec as P

REACH = 7
MESH = pl.DeviceIdType.MESH


def shifted(block, axis, distance):
    devices = range(lax.axis_size(axis))
    route = [((i - distance) % len(devices), i) for i in devices]
    return lax.ppermute(block, axis, route)


def cross_rows(left, right):
    return lax.dot_general(
        left, right, (((1,), (1,)), ((), ())), preferred_element_type=jnp.float32
    )


def cross_cols(weights, right):
    return lax.dot_general(
        weights, right, (((0,), (0,)), ((), ())), preferred_element_type=jnp.float32
    )


def band(images, texts, matches, scale, shift_bias):
    temper = scale[0]
    offset_bias = shift_bias[0]
    rows = images.shape[0]
    columns = lax.broadcasted_iota(jnp.int32, (rows, rows), 1)
    positive = (columns == matches[0][:, None]).astype(jnp.float32)

    def to_weights(total, label):
        probs = jax.nn.sigmoid(temper * total + offset_bias)
        if label is not None:
            probs = probs - label
        return probs.astype(jnp.bfloat16)

    def finish(parts, labels):
        totals = lax.psum(parts, "width")
        return tuple((to_weights(total, label) for total, label in zip(totals, labels)))

    own = finish((cross_rows(images, texts),), (positive,))[0]
    grad_image = jnp.dot(own, texts, preferred_element_type=jnp.float32)
    grad_text = cross_cols(own, images)
    for step in range(1, REACH + 1):
        lower = shifted(texts, "tour", step)
        upper = shifted(texts, "tour", -step)
        weight_low, weight_up = finish(
            (cross_rows(images, lower), cross_rows(images, upper)), (None, None)
        )
        grad_image = grad_image + jnp.dot(weight_low, lower, preferred_element_type=jnp.float32)
        grad_image = grad_image + jnp.dot(weight_up, upper, preferred_element_type=jnp.float32)
        back_low = shifted(cross_cols(weight_low, images), "tour", -step)
        back_up = shifted(cross_cols(weight_up, images), "tour", step)
        grad_text = grad_text + back_low + back_up
    return (temper * grad_image, temper * grad_text)


def kernel(
    n, m, images_in, texts_in, matches_in, scale, shift_bias, grad_image, grad_text,
    texts, matches, image_all, text_all, text_terms, term_got, hop_terms, text_got, text_own, text_sums, text_final,
    image_terms, image_sums, image_got, image_final,
    load_sem, store_sem, relay_send, quarter_send, quarter_recv, image_send, image_recv,
    plane_send, plane_recv, share_send, term_send, term_recv, hop_send, hop_recv,
    back_send, back_recv, final_send, final_recv,
):
    t, z = lax.axis_index("tour"), lax.axis_index("width")
    width, rows = images_in.shape
    cores = 2
    halves, chips = m // cores, n // cores
    half = rows // halves
    temper, offset_bias = scale[0], shift_bias[0]
    core, chip = lax.rem(t, cores), lax.div(t, cores)
    plane_core, plane_half = lax.div(z, halves), lax.rem(z, halves)
    sibling = chip * cores + (cores - 1 - core)
    slabs = [lax.rem(z + k, m) for k in range(m)]
    keepers = [lax.rem(chip + r, chips) * cores + plane_core for r in range(chips)]
    peers = [lax.rem(chip + r, chips) * cores + core for r in range(chips)]
    targets = [core * halves + h for h in range(halves)]
    same_core = lax.rem(z, cores) == core
    local = [jnp.logical_and(target == z, same_core) for target in targets]
    elsewhere = [jnp.logical_not(here) for here in local]
    landing, origin = chip * cores + lax.rem(z, cores), chip * cores + plane_core
    both_halves = range(halves)
    spans = [slice(p * half, (p + 1) * half) for p in both_halves]
    outer = jnp.logical_or(z == 0, z == m - 1)
    inner = jnp.logical_not(outer)
    low = z < halves
    partner = jnp.where(low, 1 - z, 2 * m - 3 - z)
    far_inner = jnp.where(low, halves, halves - 1)
    far_outer = jnp.where(low, m - 1, 0)
    direct = [jnp.logical_or(inner, f != far_outer) for f in slabs]
    order = (far_outer, far_inner, partner, z)
    far_start = jnp.where(low, halves, 0)
    mine = [far_start + core, halves - far_start + core]
    theirs = [far_start + cores - 1 - core, halves - far_start + cores - 1 - core]
    home = [jnp.logical_and(f == z, plane_core == core) for f in mine]
    abroad = [jnp.logical_not(here) for here in home]

    loads = [pltpu.make_async_copy(matches_in, matches, load_sem.at[2 * halves])]
    for p in both_halves:
        loads += [
            pltpu.make_async_copy(texts_in.at[:, spans[p]], texts.at[p], load_sem.at[halves + p]),
            pltpu.make_async_copy(images_in.at[:, spans[p]], image_all.at[z, p], load_sem.at[p]),
        ]
    for load in loads:
        load.start()

    def remote(src, dst, send_sem, recv_sem, device):
        return pltpu.make_async_remote_copy(
            src_ref=src, dst_ref=dst, send_sem=send_sem, recv_sem=recv_sem,
            device_id=device, device_id_type=MESH,
        )

    def arriving(dst, recv_sem):
        return remote(dst, dst, quarter_send.at[0], recv_sem, {"width": slabs[1]})

    quarter = [
        remote(
            texts.at[h], text_all.at[0, z],
            quarter_send.at[h], quarter_recv.at[z], {"tour": landing, "width": targets[h]},
        )
        for h in both_halves
    ]
    image, image_in, quarter_in, final = {}, {}, {}, {}
    plane, plane_in, share, share_in, term_out, hop, hop_in = {}, {}, {}, {}, {}, {}, {}
    for k in range(1, m):
        f = slabs[k]
        for p in both_halves:
            sent, comes = image_all.at[z, p], image_all.at[f, p]
            image[p, k] = remote(
                sent, sent, image_send.at[p, k], image_recv.at[p, z], {"width": f}
            )
            image_in[p, k] = arriving(comes, image_recv.at[p, f])
    relay, near_out, outer_out, inner_out, back_in = [], [], [], [], []
    for p in both_halves:
        passed = image_all.at[far_outer, p]
        relay.append(
            remote(
                passed, passed, relay_send.at[p], image_recv.at[p, far_outer], {"width": partner}
            )
        )

        def back(i, slot, device):
            return remote(
                image_terms.at[p, i], image_got.at[p, slot],
                back_send.at[p, i], back_recv.at[p, slot], {"width": device},
            )

        near_out.append(back(2, 2, partner))
        outer_out.append([back(0, 0, partner), back(1, 1, partner)])
        inner_out.append([back(0, 3, far_outer), back(1, 3, far_inner)])
        back_in.append([arriving(image_got.at[p, i], back_recv.at[p, i]) for i in range(4)])
    final_in = [arriving(text_final.at[h], final_recv.at[h]) for h in both_halves]
    for j in range(2):
        f, g = mine[j], theirs[j]
        quarter_in[j] = arriving(text_all.at[0, f], quarter_recv.at[f])
        term_out[j] = remote(
            text_terms.at[j], term_got.at[j], term_send.at[j], term_recv.at[j], {"tour": sibling}
        )
        final[j] = remote(
            text_sums.at[j], text_final.at[plane_half], final_send.at[j], final_recv.at[plane_half],
            {"tour": origin, "width": f},
        )
        for r in range(chips):
            plane_in[r, j] = arriving(text_all.at[r, f], plane_recv.at[r, f])
            share_in[r, j] = arriving(text_all.at[r, g], plane_recv.at[r, g])
            share[r, j] = remote(
                text_all.at[r, f], text_all.at[r, f], share_send.at[r, j], plane_recv.at[r, f],
                {"tour": sibling},
            )
            if r > 0:
                plane[r, j] = remote(
                    text_all.at[0, f], text_all.at[chips - r, f],
                    plane_send.at[r, j], plane_recv.at[chips - r, f], {"tour": peers[r]},
                )
                hop[r, j] = remote(
                    hop_terms.at[j, r - 1], text_got.at[j, chips - r - 1],
                    hop_send.at[r, j], hop_recv.at[chips - r, j], {"tour": peers[r]},
                )
                hop_in[r, j] = arriving(text_got.at[j, r - 1], hop_recv.at[r, j])

    barrier = pltpu.get_barrier_semaphore()
    for k in range(1, m):
        pl.semaphore_signal(barrier, inc=1, device_id={"width": slabs[k]}, device_id_type=MESH)
        pl.semaphore_signal(
            barrier, inc=1, device_id={"tour": sibling, "width": slabs[k]}, device_id_type=MESH
        )
    for other in peers[1:] + [sibling]:
        pl.semaphore_signal(barrier, inc=1, device_id={"tour": other}, device_id_type=MESH)
    for load in loads:
        load.wait()
    for h in both_halves:
        @pl.when(local[h])
        def _():
            text_all[0, z] = texts[h]
    pl.semaphore_wait(barrier, 2 * (m - 1) + chips)

    for h in both_halves:
        @pl.when(elsewhere[h])
        def _():
            quarter[h].start()

    def send_images(p):
        for k in (2, 1, 3):
            @pl.when(direct[k])
            def _():
                image[p, k].start()

    def pass_on(p):
        @pl.when(inner)
        def _():
            image_in[p, 2].wait_recv()
            relay[p].start()

    for j in (1, 0):
        @pl.when(abroad[j])
        def _():
            quarter_in[j].wait_recv()
        for r in range(1, chips):
            plane[r, j].start()
        share[0, j].start()

    send_images(0)
    spot = jnp.broadcast_to(matches[...].astype(jnp.float32), (half, rows)).T
    for k in range(1, m):
        @pl.when(direct[k])
        def _():
            image[0, k].wait_send()
    send_images(1)
    pass_on(0)

    for j in (1, 0):
        for r in range(1, chips):
            plane_in[r, j].wait_recv()
            share[r, j].start()
    for j in (1, 0):
        for r in range(chips):
            share_in[r, j].wait_recv()

    def text_slab(f):
        return jnp.concatenate([text_all[r, f] for r in range(chips)], axis=1)

    column = lax.broadcasted_iota(jnp.int32, (half, half), 1) + plane_half * half
    column = column.astype(jnp.float32)
    kept_label = jnp.where(core == plane_core, 1.0, 0.0)
    counts = [len([s for s in range(-REACH, REACH + 1) if s % n == d]) for d in range(n)]
    times = []
    for r in range(chips):
        distance = lax.rem(t - keepers[r] + n, n)
        count = jnp.float32(0)
        for d in range(n):
            count = jnp.where(distance == d, jnp.float32(counts[d]), count)
        times.append(count)

    def image_term(i, turned):
        return jnp.dot(text_slab(order[i]), turned, preferred_element_type=jnp.float32)

    def near_terms(p, turned):
        image_terms[p, 2] = image_term(2, turned).astype(jnp.bfloat16)
        near_out[p].start()
        image_final[:, spans[p]] = image_term(3, turned)

    weights = []
    for p in both_halves:
        total = None
        for k in range(m):
            if k == 2:
                @pl.when(outer)
                def _():
                    image_in[p, 2].wait_recv()
            elif k > 0:
                image_in[p, k].wait_recv()
            term = cross_cols(image_all[slabs[k], p], text_slab(slabs[k]))
            total = term if total is None else total + term
        probs = jax.nn.sigmoid(temper * total + offset_bias)
        pieces = []
        for r in range(chips):
            piece = probs[:, r * half : (r + 1) * half]
            if r == 0:
                piece = piece - kept_label * (column == spot[spans[p]]).astype(jnp.float32)
            pieces.append(piece.astype(jnp.bfloat16).astype(jnp.float32) * times[r])
        pieces = jnp.concatenate(pieces, axis=1)
        weights.append(pieces.astype(jnp.bfloat16))
        turned = pieces.T.astype(jnp.bfloat16)

        for i in range(2):
            term = image_term(i, turned)

            @pl.when(outer)
            def _():
                image_terms[p, i] = term.astype(jnp.bfloat16)
                outer_out[p][i].start()

            @pl.when(inner)
            def _():
                image_sums[p, i] = term
        if p == 0:
            near_terms(p, turned)
        if p == 0:
            pass_on(1)
    weights = jnp.concatenate(weights, axis=0)

    def combine(p):
        @pl.when(inner)
        def _():
            for i in range(2):
                back_in[p][i].wait_recv()
                value = image_sums[p, i] + image_got[p, i].astype(jnp.float32)
                image_terms[p, i] = value.astype(jnp.bfloat16)
                inner_out[p][i].start()

    def text_term(f):
        slab = jnp.concatenate([image_all[f, p] for p in both_halves], axis=1)
        term = jnp.dot(slab, weights, preferred_element_type=jnp.float32)
        return [term[:, r * half : (r + 1) * half] for r in range(chips)]

    for j in range(2):
        terms = text_term(theirs[j])
        for r in range(chips):
            text_terms[j, r] = terms[r].astype(jnp.bfloat16)
        term_out[j].start()
    combine(0)
    for j in range(2):
        terms = text_term(mine[j])
        term_out[j].wait_recv()
        for r in range(1, chips):
            both = terms[r] + term_got[j, r].astype(jnp.float32)
            hop_terms[j, r - 1] = both.astype(jnp.bfloat16)
            if j == 0:
                hop[r, j].start()
        text_own[j] = terms[0] + term_got[j, 0].astype(jnp.float32)

    near_terms(1, turned)
    for r in range(1, chips):
        hop[r, 0].wait_send()
    for r in range(1, chips):
        hop[r, 1].start()
    combine(1)
    for j in range(2):
        value = text_own[j]
        for r in range(1, chips):
            hop_in[r, j].wait_recv()
            value = value + text_got[j, r - 1].astype(jnp.float32)
        text_sums[j] = value

        @pl.when(home[j])
        def _():
            text_final[plane_half] = text_sums[j]

        @pl.when(abroad[j])
        def _():
            final[j].start()

    stores = []
    for p in both_halves:
        value = image_final[:, spans[p]]
        for i in (2, 3):
            back_in[p][i].wait_recv()
            value = value + image_got[p, i].astype(jnp.float32)
        image_final[:, spans[p]] = value
        stores.append(
            pltpu.make_async_copy(
                image_final.at[:, spans[p]], grad_image.at[:, spans[p]], store_sem.at[p]
            )
        )
        stores[-1].start()
    for h in both_halves:
        @pl.when(elsewhere[h])
        def _():
            final_in[h].wait_recv()
            quarter[h].wait_send()
        stores.append(
            pltpu.make_async_copy(
                text_final.at[h], grad_text.at[:, spans[h]], store_sem.at[halves + h]
            )
        )
        stores[-1].start()
    for p in both_halves:
        if p == 1:
            for k in range(1, m):
                @pl.when(direct[k])
                def _():
                    image[1, k].wait_send()
        near_out[p].wait_send()

        @pl.when(outer)
        def _():
            for copy in outer_out[p]:
                copy.wait_send()

        @pl.when(inner)
        def _():
            for copy in [relay[p]] + inner_out[p]:
                copy.wait_send()

    for r in range(1, chips):
        hop[r, 1].wait_send()
    for group in (plane, share, term_out):
        for copy in group.values():
            copy.wait_send()
    for j in range(2):
        @pl.when(abroad[j])
        def _():
            final[j].wait_send()

    for store in stores:
        store.wait()


def whole(images, texts, matches, scale, shift_bias):
    n, m = lax.axis_size("tour"), lax.axis_size("width")
    rows, width = images.shape
    chips, halves = n // 2, m // 2
    half = rows // halves
    hbm = pl.BlockSpec(memory_space=pltpu.HBM)
    smem = pl.BlockSpec(memory_space=pltpu.SMEM)
    out = jax.ShapeDtypeStruct((width, rows), jnp.float32)

    def dma(*shape):
        return pltpu.SemaphoreType.DMA(shape)

    def narrow(*shape):
        return pltpu.VMEM(shape, jnp.bfloat16)

    def wide(*shape):
        return pltpu.VMEM(shape, jnp.float32)

    grads = pl.pallas_call(
        functools.partial(kernel, n, m),
        out_shape=(out, out),
        in_specs=[hbm, hbm, hbm, smem, smem],
        out_specs=(hbm, hbm),
        scratch_shapes=[
            narrow(halves, width, half), pltpu.VMEM((1, rows), jnp.int32),
            narrow(m, halves, width, half),
            narrow(chips, m, width, half), narrow(2, chips, width, half),
            narrow(2, chips, width, half), narrow(2, chips - 1, width, half),
            narrow(2, chips - 1, width, half),
            wide(2, width, half), wide(2, width, half), wide(halves, width, half),
            narrow(halves, 3, width, half), wide(halves, 2, width, half),
            narrow(halves, 4, width, half), wide(width, rows),
            dma(2 * halves + 1), dma(2 * halves), dma(halves), dma(halves), dma(m), dma(halves, m), dma(halves, m),
            dma(chips, 2), dma(chips, m), dma(chips, 2), dma(2), dma(2), dma(chips, 2), dma(chips, 2),
            dma(halves, 3), dma(halves, 4), dma(2), dma(halves),
        ],
        compiler_params=pltpu.CompilerParams(
            collective_id=0, has_side_effects=True, vmem_limit_bytes=60 * 1024 * 1024
        ),
    )(images.T, texts.T, matches, scale, shift_bias)
    return tuple(scale[0] * grad.T for grad in grads)


def solution(mesh):
    placed = (P("tour", "width"), P("tour", "width"), P("tour", None), P(), P())
    n, m = mesh.shape["tour"], mesh.shape["width"]
    body = whole if n <= 2 * REACH + 1 and n % 2 == 0 and m == 4 else band
    return jax.shard_map(
        body,
        mesh=mesh,
        in_specs=placed,
        out_specs=(P("tour", "width"), P("tour", "width")),
        check_vma=False,
    )
```
